32 devices in a mesh: rep: 2 (over x), store: 8 (over z, y), tensor: 2 (over core).
Axes of the slice: x: 2, y: 2, z: 4, core: 2. Of those that a mesh axis runs over, the one named last changes fastest.
Arguments:
- queries: bfloat16 [384, 4, 32, 128], P(('rep', 'store'), None, 'tensor'), parts along dimension 0, may hold values from -24 to 24
- kv_cache: bfloat16 [2, 384, 4, 256, 128], P(None, ('rep', 'store'), 'tensor'), parts along dimension 1, may hold values from -12 to 12
- new_kv: bfloat16 [2, 384, 4, 4, 128], P(None, ('rep', 'store'), None, 'tensor'), parts along dimension 1, may hold values from -12 to 12
- lengths: int32 [384], P(('rep', 'store')), parts along dimension 0, may hold values from 1 to 256, 24576 in all
- adapter_ids: int32 [384], P(('rep', 'store')), parts along dimension 0, may hold values from 0 to 63, as said below
- place: int32 [128], P('rep'), parts along dimension 0, may hold values from 0 to 63, as said below
- ranks: int32 [128], P('rep'), parts along dimension 0, may hold values from 4 to 64
- w_out: bfloat16 [4096, 4096], P('tensor'), may hold values from -0.09375 to 0.09375
- a_store: bfloat16 [128, 4096, 64], P(('rep', 'store'), 'tensor'), parts along dimension 0, may hold values from -0.09375 to 0.09375
- b_store: bfloat16 [128, 64, 4096], P(('rep', 'store'), None, 'tensor'), parts along dimension 0, may hold values from -0.75 to 0.75
Outputs:
- mixed: bfloat16 [384, 4, 4096], P(('rep', 'store'), None, 'tensor'), parts along dimension 0
The draws below stay inside these ranges and needn't reach their ends.
There are 2 independent parts, one for each index of `rep`. The reference program is written for one: setup_inputs(seed, part) draws one part's arguments, and reference() takes and returns one part's arrays. A program takes and returns all parts, laid end to end along the dimension named above; an argument that names none is the same for every part. Nothing has to cross between parts.
Inputs may be any that keep to these rules, and one draw needn't show every extreme that they name: Adapter a's factor blocks stand at position place[a] of a_store and b_store; each position once. `adapter_ids`: among the 24 requests of one group, at most 3 use adapters placed with one owner (place // 8), and those name at most 2 distinct adapters; both bounds are reached in every group.
All inputs are finite; a program needn't handle non-finite values. No bound on the sum of `lengths` on one device may be relied on, other than what follows from the above.
Results may differ from the reference program's by a relative error of at most 0.008.
Values may be sent and summed in bfloat16 or wider, within the bound.
No kernel may reach another device: no remote copies, remote signals or barrier semaphores. Data moves between devices by JAX's collectives and lax.ppermute only.
A program may use at most 128 MiB of HBM per device.

```python
import math
import jax
import jax.numpy as jnp
import numpy as np
from jax import lax

MODEL_WIDTH = 4096
HEADS = 32
KVHEADS = 4
HDIM = 128
RP = 64
NEW_POSITIONS = 4
ACAP = 2
QCAP = 3
R_DEV = 24
CACHE = 256
ADP_DEV = 8
REQUEST_TOTAL = 192
ADAPTERS = 64
HD = 4096
N_STORE = 8


def adapter_layout(key):
    placement = jax.random.permutation(jax.random.fold_in(key, 11), ADAPTERS).astype(jnp.int32)
    inverse = jnp.argsort(placement).astype(jnp.int32)
    owner_heat = jax.random.randint(jax.random.fold_in(key, 12), (N_STORE,), 0, 4)
    seat_count = N_STORE * QCAP
    seat_index = jnp.arange(seat_count, dtype=jnp.int32)
    seat_owner = seat_index // QCAP
    noise_draw = jax.random.randint(jax.random.fold_in(key, 13), (N_STORE, seat_count), 0, 4096)
    hot_owner = jax.random.randint(jax.random.fold_in(key, 14), (N_STORE,), 0, N_STORE)
    seat_score = noise_draw // (1 + 3 * owner_heat[seat_owner])[None, :]
    seat_score = jnp.where(seat_owner[None, :] == hot_owner[:, None], -1, seat_score)
    seat_score = seat_score * seat_count + seat_index[None, :]
    chosen = jnp.argsort(seat_score, axis=1)[:, :R_DEV].astype(jnp.int32)
    owner_of = chosen // QCAP
    turn_of = chosen % QCAP
    pick_of = jax.random.randint(jax.random.fold_in(key, 15), (N_STORE, R_DEV), 0, ACAP)
    forced = (owner_of == hot_owner[:, None]) & (turn_of < ACAP)
    pick_of = jnp.where(forced, turn_of, pick_of)
    start_slot = jax.random.randint(jax.random.fold_in(key, 16), (N_STORE, N_STORE), 0, ADP_DEV)
    begin_slot = jnp.take_along_axis(start_slot, owner_of, axis=1)
    slot_of = (begin_slot + pick_of) % ADP_DEV
    request_ids = inverse[owner_of * ADP_DEV + slot_of]
    shuffle_score = jax.random.randint(jax.random.fold_in(key, 17), (N_STORE, R_DEV), 0, 4096)
    shuffle_score = shuffle_score * R_DEV + jnp.arange(R_DEV, dtype=jnp.int32)[None, :]
    shuffle = jnp.argsort(shuffle_score, axis=1)
    request_ids = jnp.take_along_axis(request_ids, shuffle, axis=1)
    return (placement, request_ids.reshape(REQUEST_TOTAL).astype(jnp.int32))


def draw_place(key, part):
    return adapter_layout(key)[0]


def draw_adapter_ids(key, part):
    return adapter_layout(key)[1]


def draw_kv_cache(key, part):
    key = jax.random.fold_in(key, 21)
    first_key, second_key = jax.random.split(key)
    shape = (REQUEST_TOTAL, KVHEADS, CACHE, HDIM)
    key_rows = jnp.clip(jax.random.normal(first_key, shape, jnp.float32), -4.0, 4.0)
    value_rows = 3.0 * jnp.clip(jax.random.normal(second_key, shape, jnp.float32), -4.0, 4.0)
    return jnp.stack([key_rows, value_rows]).astype(jnp.bfloat16)


def draw_new_kv(key, part):
    key = jax.random.fold_in(key, 22)
    first_key, second_key = jax.random.split(key)
    shape = (REQUEST_TOTAL, NEW_POSITIONS, KVHEADS, HDIM)
    key_rows = jnp.clip(jax.random.normal(first_key, shape, jnp.float32), -4.0, 4.0)
    value_rows = 3.0 * jnp.clip(jax.random.normal(second_key, shape, jnp.float32), -4.0, 4.0)
    return jnp.stack([key_rows, value_rows]).astype(jnp.bfloat16)


def draw_queries(key, part):
    key = jax.random.fold_in(key, 23)
    first_key = jax.random.fold_in(key, 0)
    shape = (REQUEST_TOTAL, NEW_POSITIONS, HEADS, HDIM)
    result = 1.5 * jnp.clip(jax.random.normal(first_key, shape, jnp.float32), -4.0, 4.0)
    return result.astype(jnp.bfloat16)


def touch_ends(values, own_key, low, largest):
    spot = [jax.random.randint(jax.random.fold_in(own_key, axis), (), 0, length) for axis, length in enumerate(values.shape)]
    widest = values.shape.index(max(values.shape))
    next_to = spot[:widest] + [(spot[widest] + 1) % values.shape[widest]] + spot[widest + 1:]
    return values.at[tuple(spot)].set(low).at[tuple(next_to)].set(largest)


def steps_of(own_key, dims, shards, least, largest):
    factor_of, own = 1.0, jax.random.fold_in(own_key, 6)
    for position, shards_of in shards:
        heights = jnp.exp(jax.random.uniform(jax.random.fold_in(own, position), (shards_of,), jnp.float32, least / len(shards), largest / len(shards)))
        factor_of = factor_of * jnp.repeat(heights, dims[position] // shards_of).reshape([-1 if axis == position else 1 for axis in range(len(dims))])
    return factor_of


def split_up(count, total, bound, skew):
    loads = [(1 << 20) // math.isqrt(rank ** skew) + 1 for rank in range(2, count + 1)]
    surplus, given = total - bound - (count - 1), [1] * (count - 1)
    while surplus > 0:
        free = [i for i in range(count - 1) if given[i] < bound]
        mass, left = sum([loads[i] for i in free]), surplus
        for i in free:
            more = min(bound - given[i], max(1, left * loads[i] // mass), surplus)
            given[i] = given[i] + more
            surplus = surplus - more
    return np.array([bound] + given)


def uneven_parts(key, number_of, total, limit, skew):
    if number_of == 2:
        one = jax.random.randint(key, (), max(1, total - limit), min(limit, total - 1) + 1)
        return jnp.stack([one, total - one])
    sizes = jnp.asarray(split_up(number_of, total, limit, skew), jnp.int32)
    pairs = (number_of - 1) // 2
    donor, taker = sizes[1:1 + 2 * pairs:2], sizes[2:2 + 2 * pairs:2]
    room = jnp.minimum(donor - 1, limit - taker)
    shifted = jax.random.randint(jax.random.fold_in(key, 1), (pairs,), 0, 1 << 20) % (room + 1)
    sizes = sizes.at[1:1 + 2 * pairs:2].set(donor - shifted).at[2:2 + 2 * pairs:2].set(taker + shifted)
    return sizes[jax.random.permutation(jax.random.fold_in(key, 2), number_of)]


def noise(own_key, extent, scale, reach, cuts=(), kind=jnp.bfloat16):
    values = jax.random.normal(own_key, extent, jnp.float32) * scale
    if len(cuts) > 0:
        values = steps_of(own_key, extent, cuts, -0.22, 0.18) * values
    return jnp.clip(values, min=-reach, max=reach).astype(kind)


def setup_inputs(seed: int = 0, part: int = 0) -> dict:
    key_of = jax.random.split(jax.random.key(seed), 11)
    part_keys = jax.random.split(jax.random.fold_in(key_of[10], part), 11)
    return {
        "queries": draw_queries(jax.random.fold_in(jax.random.fold_in(key_of[10], part), 71), part),
        "kv_cache": draw_kv_cache(jax.random.fold_in(jax.random.fold_in(key_of[10], part), 71), part),
        "new_kv": draw_new_kv(jax.random.fold_in(jax.random.fold_in(key_of[10], part), 71), part),
        "lengths": uneven_parts(part_keys[3], REQUEST_TOTAL, REQUEST_TOTAL * CACHE // 2, CACHE, 2).astype(jnp.int32),
        "adapter_ids": draw_adapter_ids(jax.random.fold_in(jax.random.fold_in(key_of[10], part), 71), part),
        "place": draw_place(jax.random.fold_in(jax.random.fold_in(key_of[10], part), 71), part),
        "ranks": touch_ends(jax.random.randint(part_keys[6], (ADAPTERS,), 4, RP + 1), jax.random.fold_in(part_keys[6], 1), 4, RP).astype(jnp.int32),
        "w_out": noise(key_of[7], (HD, MODEL_WIDTH), HD ** -0.5, 0.09375, ((0, 2),)),
        "a_store": noise(part_keys[8], (ADAPTERS, HD, RP), HD ** -0.5, 0.09375, ((0, 8), (1, 2))),
        "b_store": noise(part_keys[9], (ADAPTERS, RP, MODEL_WIDTH), RP ** -0.5, 0.75, ((0, 8), (2, 2))),
    }


adapter_scale = 8.0

def rank_factor(request_rank, width):
    column_indices = jnp.arange(width, dtype=jnp.int32)
    rank_as_real = request_rank.astype(jnp.float32)[..., None]
    return jnp.where(column_indices < request_rank[..., None], adapter_scale / jnp.sqrt(rank_as_real), 0.0)

def reference(queries, kv_cache, new_kv, lengths, adapter_ids, place, ranks, w_out, a_store, b_store):
    group_heads = HEADS // KVHEADS
    grouped = queries.astype(jnp.float32).reshape(REQUEST_TOTAL, NEW_POSITIONS, KVHEADS, group_heads, HDIM)
    key_rows = kv_cache[0].astype(jnp.float32)
    value_rows = kv_cache[1].astype(jnp.float32)
    new_keys = new_kv[0].astype(jnp.float32)
    new_values = new_kv[1].astype(jnp.float32)
    score_scale = 1.0 / math.sqrt(HDIM)
    cached = jnp.einsum('rsngd,rncd->rsngc', grouped, key_rows) * score_scale
    visible = jnp.arange(CACHE, dtype=jnp.int32)[None, :] < lengths[:, None]
    cached = jnp.where(visible[:, None, None, None, :], cached, -jnp.inf)
    new_scores = jnp.einsum('rsngd,rtnd->rsngt', grouped, new_keys) * score_scale
    causal = jnp.arange(NEW_POSITIONS)[:, None] >= jnp.arange(NEW_POSITIONS)[None, :]
    new_scores = jnp.where(causal[None, :, None, None, :], new_scores, -jnp.inf)
    scores = jnp.concatenate([cached, new_scores], axis=-1)
    row_max = lax.optimization_barrier(jnp.max(scores, axis=-1, keepdims=True))
    exponent = jnp.exp(scores - row_max)
    weights_bf = (exponent / lax.optimization_barrier(jnp.sum(exponent, axis=-1, keepdims=True))).astype(jnp.bfloat16)
    weights_f = weights_bf.astype(jnp.float32)
    attended = jnp.einsum('rsngc,rncd->rsngd', weights_f[..., :CACHE], value_rows)
    attended = attended + jnp.einsum('rsngt,rtnd->rsngd', weights_f[..., CACHE:], new_values)
    attended = attended.reshape(REQUEST_TOTAL, NEW_POSITIONS, HD).astype(jnp.bfloat16)
    plain_projection_sum = jnp.dot(attended.reshape(REQUEST_TOTAL * NEW_POSITIONS, HD), w_out, preferred_element_type=jnp.float32)
    location = place[adapter_ids]
    request_rank = ranks[adapter_ids]
    first_req = a_store[location].astype(jnp.float32)
    partial_value = jnp.einsum('rsh,rhk->rsk', attended.astype(jnp.float32), first_req)
    narrow_product = (partial_value * rank_factor(request_rank, RP)[:, None, :]).astype(jnp.bfloat16)
    second_request = b_store[location].astype(jnp.float32)
    adapter_update = jnp.einsum('hpx,hxg->hpg', narrow_product.astype(jnp.float32), second_request).astype(jnp.bfloat16)
    mixed = plain_projection_sum.reshape(REQUEST_TOTAL, NEW_POSITIONS, MODEL_WIDTH) + adapter_update.astype(jnp.float32)
    return mixed.astype(jnp.bfloat16)
```

```python
import math

import jax
import jax.numpy as jnp
from jax import lax
from jax.sharding import PartitionSpec as P

QCAP = 3


adapter_scale = 8.0


def rank_factor(request_rank, width):
    column_indices = jnp.arange(width, dtype=jnp.int32)
    rank_as_real = request_rank.astype(jnp.float32)[..., None]
    return jnp.where(
        column_indices < request_rank[..., None], adapter_scale / jnp.sqrt(rank_as_real), 0.0
    )


def lookup(table, index):
    hits = index[:, None] == jnp.arange(table.shape[0], dtype=jnp.int32)[None, :]
    return jnp.sum(jnp.where(hits, table[None, :], 0), axis=1)


def attend(queries, kv_cache, new_kv, lengths):
    request_count, step_count, head_count, head_size = queries.shape
    key_heads = kv_cache.shape[2]
    cache_slots = kv_cache.shape[3]
    grouped = queries.reshape(
        request_count, step_count, key_heads, head_count // key_heads, head_size
    )
    score_scale = 1.0 / math.sqrt(head_size)
    cached = (
        jnp.einsum("rsngd,rncd->rsngc", grouped, kv_cache[0], preferred_element_type=jnp.float32)
        * score_scale
    )
    visible = jnp.arange(cache_slots, dtype=jnp.int32)[None, :] < lengths[:, None]
    cached = jnp.where(visible[:, None, None, None, :], cached, -jnp.inf)
    new_scores = (
        jnp.einsum("rsngd,rtnd->rsngt", grouped, new_kv[0], preferred_element_type=jnp.float32)
        * score_scale
    )
    causal = jnp.arange(step_count)[:, None] >= jnp.arange(step_count)[None, :]
    new_scores = jnp.where(causal[None, :, None, None, :], new_scores, -jnp.inf)
    scores = jnp.concatenate([cached, new_scores], axis=-1)
    row_max = jnp.max(scores, axis=-1, keepdims=True)
    exponent = jnp.exp(scores - row_max)
    weights_bf = (exponent / jnp.sum(exponent, axis=-1, keepdims=True)).astype(jnp.bfloat16)
    attended = jnp.einsum(
        "rsngc,rncd->rsngd",
        weights_bf[..., :cache_slots],
        kv_cache[1],
        preferred_element_type=jnp.float32,
    )
    attended = attended + jnp.einsum(
        "rsngt,rtnd->rsngd",
        weights_bf[..., cache_slots:],
        new_kv[1],
        preferred_element_type=jnp.float32,
    )
    return attended.reshape(request_count, step_count, head_count * head_size).astype(jnp.bfloat16)


def local(queries, kv_cache, new_kv, lengths, adapter_ids, place, ranks, w_out, a_store, b_store):
    request_count, step_count = (queries.shape[0], queries.shape[1])
    owners = lax.axis_size("store")
    per_owner, feature_half, rank_width = a_store.shape
    out_half = b_store.shape[2]
    location = lookup(place, adapter_ids)
    owner_of = location // per_owner
    slot_of = location % per_owner
    order_index = jnp.arange(request_count, dtype=jnp.int32)
    earlier = order_index[None, :] < order_index[:, None]
    same_owner = owner_of[:, None] == owner_of[None, :]
    turn = jnp.sum(same_owner & earlier, axis=1)
    seat = owner_of * QCAP + turn
    seats = owners * QCAP
    pick = seat[:, None] == jnp.arange(seats, dtype=jnp.int32)[None, :]
    slot_sent = jnp.sum(jnp.where(pick, slot_of[:, None], 0), axis=0)
    pick = pick.astype(jnp.bfloat16)

    attended = attend(queries, kv_cache, new_kv, lengths)
    sent = jnp.einsum(
        "rq,rsf->qsf", pick, attended, preferred_element_type=jnp.float32
    ).astype(jnp.bfloat16)
    sent = sent.reshape(owners, QCAP * step_count * feature_half // 128, 128)
    note = jnp.broadcast_to(
        slot_sent.reshape(owners, QCAP, 1), (owners, QCAP, 128)
    ).astype(jnp.bfloat16)
    note = jnp.pad(note, ((0, 0), (0, 16 - QCAP), (0, 0)))
    sent = jnp.concatenate([sent, note], axis=1)
    got = lax.all_to_all(sent, "store", split_axis=0, concat_axis=0, tiled=True)

    partial_out = jnp.dot(
        attended.reshape(request_count * step_count, feature_half),
        w_out,
        preferred_element_type=jnp.float32,
    )
    plain_projection_sum = lax.psum_scatter(
        partial_out, "tensor", scatter_dimension=1, tiled=True
    )

    body = QCAP * step_count * feature_half // 128
    rows = got[:, :body].reshape(seats * step_count, feature_half)
    slots = got[:, body : body + QCAP, 0].astype(jnp.int32).reshape(seats)
    mine = slots[:, None] == jnp.arange(per_owner, dtype=jnp.int32)[None, :]
    mine = jnp.repeat(mine, step_count, axis=0)
    here = lax.axis_index("store") * per_owner + jnp.arange(per_owner, dtype=jnp.int32)
    slot_rank = jnp.sum(jnp.where(here[:, None] == place[None, :], ranks[None, :], 0), axis=1)
    factor = rank_factor(slot_rank, rank_width)
    every = jnp.einsum("mf,pfk->mpk", rows, a_store, preferred_element_type=jnp.float32)
    partial_value = jnp.sum(jnp.where(mine[:, :, None], every, 0.0), axis=1)
    summed = lax.psum(partial_value, "tensor")
    spread = jnp.where(mine[:, :, None], summed[:, None, :] * factor[None], 0.0).astype(jnp.bfloat16)
    update = jnp.einsum(
        "mpk,pkg->mg", spread, b_store, preferred_element_type=jnp.float32
    ).astype(jnp.bfloat16)
    back = lax.all_to_all(
        update.reshape(owners, body, 128), "store", split_axis=0, concat_axis=0, tiled=True
    )
    back = back.reshape(seats, step_count, out_half)
    adapter_update = jnp.einsum("rq,qsg->rsg", pick, back, preferred_element_type=jnp.float32)
    plain_projection_sum = plain_projection_sum.reshape(request_count, step_count, out_half)
    return (plain_projection_sum + adapter_update).astype(jnp.bfloat16)


def solution(mesh):
    return jax.shard_map(
        local,
        mesh=mesh,
        in_specs=(
            P(("rep", "store"), None, "tensor", None),
            P(None, ("rep", "store"), "tensor", None, None),
            P(None, ("rep", "store"), None, "tensor", None),
            P(("rep", "store")),
            P(("rep", "store")),
            P("rep"),
            P("rep"),
            P("tensor", None),
            P(("rep", "store"), "tensor", None),
            P(("rep", "store"), None, "tensor"),
        ),
        out_specs=P(("rep", "store"), None, "tensor"),
        check_vma=False,
    )
```

```python
import math

import jax
import jax.numpy as jnp
from jax import lax
from jax.sharding import PartitionSpec as P

QCAP = 3


adapter_scale = 8.0


def rank_factor(request_rank, width):
    column_indices = jnp.arange(width, dtype=jnp.int32)
    rank_as_real = request_rank.astype(jnp.float32)[..., None]
    return jnp.where(
        column_indices < request_rank[..., None], adapter_scale / jnp.sqrt(rank_as_real), 0.0
    )


def lookup(table, index):
    hits = index[:, None] == jnp.arange(table.shape[0], dtype=jnp.int32)[None, :]
    return jnp.sum(jnp.where(hits, table[None, :], 0), axis=1)


def attend(queries, kv_cache, new_kv, lengths):
    request_count, step_count, head_count, head_size = queries.shape
    key_heads = kv_cache.shape[2]
    cache_slots = kv_cache.shape[3]
    grouped = queries.reshape(
        request_count, step_count, key_heads, head_count // key_heads, head_size
    )
    score_scale = 1.0 / math.sqrt(head_size)
    cached = (
        jnp.einsum("rsngd,rncd->rsngc", grouped, kv_cache[0], preferred_element_type=jnp.float32)
        * score_scale
    )
    visible = jnp.arange(cache_slots, dtype=jnp.int32)[None, :] < lengths[:, None]
    cached = jnp.where(visible[:, None, None, None, :], cached, -jnp.inf)
    new_scores = (
        jnp.einsum("rsngd,rtnd->rsngt", grouped, new_kv[0], preferred_element_type=jnp.float32)
        * score_scale
    )
    causal = jnp.arange(step_count)[:, None] >= jnp.arange(step_count)[None, :]
    new_scores = jnp.where(causal[None, :, None, None, :], new_scores, -jnp.inf)
    scores = jnp.concatenate([cached, new_scores], axis=-1)
    row_max = jnp.max(scores, axis=-1, keepdims=True)
    exponent = jnp.exp(scores - row_max)
    weights_bf = (exponent / jnp.sum(exponent, axis=-1, keepdims=True)).astype(jnp.bfloat16)
    attended = jnp.einsum(
        "rsngc,rncd->rsngd",
        weights_bf[..., :cache_slots],
        kv_cache[1],
        preferred_element_type=jnp.float32,
    )
    attended = attended + jnp.einsum(
        "rsngt,rtnd->rsngd",
        weights_bf[..., cache_slots:],
        new_kv[1],
        preferred_element_type=jnp.float32,
    )
    return attended.reshape(request_count, step_count, head_count * head_size).astype(jnp.bfloat16)


def local(queries, kv_cache, new_kv, lengths, adapter_ids, place, ranks, w_out, a_store, b_store):
    request_count, step_count = (queries.shape[0], queries.shape[1])
    owners = lax.axis_size("store")
    per_owner, feature_half, rank_width = a_store.shape
    out_half = b_store.shape[2]
    location = lookup(place, adapter_ids)
    owner_of = location // per_owner
    slot_of = location % per_owner
    order_index = jnp.arange(request_count, dtype=jnp.int32)
    earlier = order_index[None, :] < order_index[:, None]
    same_owner = owner_of[:, None] == owner_of[None, :]
    turn = jnp.sum(same_owner & earlier, axis=1)
    seat = owner_of * QCAP + turn
    seats = owners * QCAP
    pick = seat[:, None] == jnp.arange(seats, dtype=jnp.int32)[None, :]
    slot_sent = jnp.sum(jnp.where(pick, slot_of[:, None], 0), axis=0)
    pick = pick.astype(jnp.bfloat16)

    attended = attend(queries, kv_cache, new_kv, lengths)
    sent = jnp.einsum(
        "rq,rsf->qsf", pick, attended, preferred_element_type=jnp.float32
    ).astype(jnp.bfloat16)
    sent = sent.reshape(owners, QCAP * step_count * feature_half // 128, 128)
    note = jnp.broadcast_to(
        slot_sent.reshape(owners, QCAP, 1), (owners, QCAP, 128)
    ).astype(jnp.bfloat16)
    note = jnp.pad(note, ((0, 0), (0, 16 - QCAP), (0, 0)))
    sent = jnp.concatenate([sent, note], axis=1)
    got = lax.all_to_all(sent, "store", split_axis=0, concat_axis=0, tiled=True)

    held, _ = lax.optimization_barrier((attended, sent))
    partial_out = jnp.dot(
        held.reshape(request_count * step_count, feature_half),
        w_out,
        preferred_element_type=jnp.float32,
    )
    got, partial_out = lax.optimization_barrier((got, partial_out))
    core = lax.axis_index("tensor")
    cores = lax.axis_size("tensor")
    plain_projection_sum = lax.dynamic_slice_in_dim(partial_out, core * out_half, out_half, 1)
    for step in range(1, cores):
        target = (core + step) % cores
        share = lax.dynamic_slice_in_dim(partial_out, target * out_half, out_half, 1)
        plain_projection_sum = plain_projection_sum + lax.ppermute(
            share, "tensor", [(k, (k + step) % cores) for k in range(cores)]
        )

    body = QCAP * step_count * feature_half // 128
    rows = got[:, :body].reshape(seats * step_count, feature_half)
    slots = got[:, body : body + QCAP, 0].astype(jnp.int32).reshape(seats)
    mine = slots[:, None] == jnp.arange(per_owner, dtype=jnp.int32)[None, :]
    mine = jnp.repeat(mine, step_count, axis=0)
    here = lax.axis_index("store") * per_owner + jnp.arange(per_owner, dtype=jnp.int32)
    slot_rank = jnp.sum(jnp.where(here[:, None] == place[None, :], ranks[None, :], 0), axis=1)
    factor = rank_factor(slot_rank, rank_width)
    every = jnp.einsum("mf,pfk->mpk", rows, a_store, preferred_element_type=jnp.float32)
    partial_value = jnp.sum(jnp.where(mine[:, :, None], every, 0.0), axis=1)
    summed = partial_value
    for step in range(1, cores):
        summed = summed + lax.ppermute(
            partial_value, "tensor", [(k, (k + step) % cores) for k in range(cores)]
        )
    spread = jnp.where(mine[:, :, None], summed[:, None, :] * factor[None], 0.0).astype(jnp.bfloat16)
    update = jnp.einsum(
        "mpk,pkg->mg", spread, b_store, preferred_element_type=jnp.float32
    ).astype(jnp.bfloat16)
    back = lax.all_to_all(
        update.reshape(owners, body, 128), "store", split_axis=0, concat_axis=0, tiled=True
    )
    back = back.reshape(seats, step_count, out_half)
    adapter_update = jnp.einsum("rq,qsg->rsg", pick, back, preferred_element_type=jnp.float32)
    plain_projection_sum = plain_projection_sum.reshape(request_count, step_count, out_half)
    return (plain_projection_sum + adapter_update).astype(jnp.bfloat16)


def solution(mesh):
    return jax.shard_map(
        local,
        mesh=mesh,
        in_specs=(
            P(("rep", "store"), None, "tensor", None),
            P(None, ("rep", "store"), "tensor", None, None),
            P(None, ("rep", "store"), None, "tensor", None),
            P(("rep", "store")),
            P(("rep", "store")),
            P("rep"),
            P("rep"),
            P("tensor", None),
            P(("rep", "store"), "tensor", None),
            P(("rep", "store"), None, "tensor"),
        ),
        out_specs=P(("rep", "store"), None, "tensor"),
        check_vma=False,
    )
```

```python
import functools
import math

import jax
import jax.numpy as jnp
from jax import lax
from jax.experimental import pallas as pl
from jax.experimental.pallas import tpu as pltpu
from jax.sharding import PartitionSpec as P

QCAP = 3
LANES = 128
NOTE = 16
ATTEND_VMEM = 60 * 1024 * 1024
SMALL_VMEM = 8 * 1024 * 1024
BATCH = 4

adapter_scale = 8.0


def rank_factor(request_rank, width):
    column_indices = jnp.arange(width, dtype=jnp.int32)
    rank_as_real = request_rank.astype(jnp.float32)[..., None]
    return jnp.where(
        column_indices < request_rank[..., None], adapter_scale / jnp.sqrt(rank_as_real), 0.0
    )


def dot(left, right, contract=(1, 0)):
    return lax.dot_general(
        left, right, (((contract[0],), (contract[1],)), ((), ())), preferred_element_type=jnp.float32
    )


def attend_kernel(
    steps, heads, per_owner,
    lengths, adapter_ids, place,
    q_ref, kv_ref, new_ref,
    attended_ref, sent_ref, seat_ref,
    taken, slots,
):
    owners = taken.shape[0]
    seats = owners * QCAP
    requests = seat_ref.shape[0]
    batch, rows, width = q_ref.shape
    slots_in_cache = kv_ref.shape[3]
    group = heads // 2
    step = pl.program_id(0)

    @pl.when(step == 0)
    def _():
        for owner in range(owners):
            taken[owner] = 0
        for seat in range(seats):
            slots[seat] = 0
        if seats > requests:
            sent_ref[...] = jnp.zeros_like(sent_ref)

    row = lax.broadcasted_iota(jnp.int32, (rows, width), 0)
    first = (row // group) % 2 == 0
    new_count = new_ref.shape[2]
    new_row = lax.broadcasted_iota(jnp.int32, (rows, new_count), 0)
    new_column = lax.broadcasted_iota(jnp.int32, (rows, new_count), 1)
    new_seen = (new_column // 2 <= new_row // heads) & (new_column % 2 == (new_row // group) % 2)
    column = lax.broadcasted_iota(jnp.int32, (rows, slots_in_cache), 1)
    scale = 1.0 / math.sqrt(width)

    cached, fresh = [], []
    for j in range(batch):
        q = q_ref[j]
        q_wide = q.astype(jnp.float32)
        both = jnp.concatenate(
            [jnp.where(first, q_wide, 0.0), jnp.where(first, 0.0, q_wide)], axis=1
        ).astype(jnp.bfloat16)
        keys = jnp.concatenate([kv_ref[0, j, 0], kv_ref[0, j, 1]], axis=1)
        scores = dot(both, keys, (1, 1)) * scale
        cached.append(jnp.where(column < lengths[step * batch + j], scores, -jnp.inf))
        scores = dot(q, new_ref[0, j], (1, 1)) * scale
        fresh.append(jnp.where(new_seen, scores, -jnp.inf))
    tops = [
        jnp.maximum(jnp.max(a, axis=1, keepdims=True), jnp.max(b, axis=1, keepdims=True))
        for a, b in zip(cached, fresh)
    ]
    cached = [jnp.exp(a - top) for a, top in zip(cached, tops)]
    fresh = [jnp.exp(b - top) for b, top in zip(fresh, tops)]
    sums = [
        1.0 / (jnp.sum(a, axis=1, keepdims=True) + jnp.sum(b, axis=1, keepdims=True))
        for a, b in zip(cached, fresh)
    ]
    cached = [(a * inv).astype(jnp.bfloat16) for a, inv in zip(cached, sums)]
    fresh = [(b * inv).astype(jnp.bfloat16) for b, inv in zip(fresh, sums)]
    for j in range(batch):
        values = jnp.concatenate([kv_ref[1, j, 0], kv_ref[1, j, 1]], axis=1)
        both = dot(cached[j], values)
        result = jnp.where(first, both[:, :width], both[:, width:]) + dot(fresh[j], new_ref[1, j])
        result = result.astype(jnp.bfloat16)
        request = step * batch + j
        location = place[adapter_ids[request]]
        owner = location // per_owner
        turn = taken[owner]
        taken[owner] = turn + 1
        slots[owner * QCAP + turn] = location % per_owner
        seat_ref[request] = owner * QCAP + turn
        attended_ref[j] = result
        sent_ref[owner, pl.ds(pl.multiple_of(turn * rows, rows), rows), :] = result

    @pl.when(step == steps - 1)
    def _():
        note_row = lax.broadcasted_iota(jnp.int32, (NOTE, width), 0)
        per_seat = rows // heads
        for owner in range(owners):
            note = jnp.zeros((NOTE, width), jnp.int32)
            for turn in range(QCAP):
                note = jnp.where(note_row // per_seat == turn, slots[owner * QCAP + turn], note)
            sent_ref[owner, QCAP * rows :, :] = note.astype(jnp.float32).astype(jnp.bfloat16)


def attend(queries, kv_cache, new_kv, lengths, adapter_ids, place, owners, per_owner):
    requests, step_count, heads, width = queries.shape
    cache_slots = kv_cache.shape[3]
    rows = step_count * heads
    new_rows = new_kv.shape[2] * new_kv.shape[3]
    batch = BATCH if requests % BATCH == 0 else 1
    steps = requests // batch
    body = QCAP * rows + NOTE
    return pl.pallas_call(
        functools.partial(attend_kernel, steps, heads, per_owner),
        grid_spec=pltpu.PrefetchScalarGridSpec(
            num_scalar_prefetch=3,
            grid=(steps,),
            in_specs=[
                pl.BlockSpec((batch, rows, width), lambda i, *_: (i, 0, 0)),
                pl.BlockSpec((2, batch, 2, cache_slots, width), lambda i, *_: (0, i, 0, 0, 0)),
                pl.BlockSpec((2, batch, new_rows, width), lambda i, *_: (0, i, 0, 0)),
            ],
            out_specs=[
                pl.BlockSpec((batch, rows, width), lambda i, *_: (i, 0, 0)),
                pl.BlockSpec((owners, body, width), lambda i, *_: (0, 0, 0)),
                pl.BlockSpec(memory_space=pltpu.SMEM),
            ],
            scratch_shapes=[
                pltpu.SMEM((owners,), jnp.int32),
                pltpu.SMEM((owners * QCAP,), jnp.int32),
            ],
        ),
        out_shape=[
            jax.ShapeDtypeStruct((requests, rows, width), jnp.bfloat16),
            jax.ShapeDtypeStruct((owners, body, width), jnp.bfloat16),
            jax.ShapeDtypeStruct((requests,), jnp.int32),
        ],
        compiler_params=pltpu.CompilerParams(
            dimension_semantics=("arbitrary",), vmem_limit_bytes=ATTEND_VMEM
        ),
        cost_estimate=pl.CostEstimate(
            flops=4 * requests * rows * cache_slots * width * 2,
            bytes_accessed=kv_cache.size * 2 + 4 * queries.size,
            transcendentals=requests * rows * cache_slots,
        ),
        name="attend",
    )(
        lengths,
        adapter_ids,
        place,
        queries.reshape(requests, rows, width),
        kv_cache,
        new_kv.reshape(2, requests, new_rows, width),
    )


def low_kernel(seats, steps, got_ref, a_ref, low_ref, slot_ref, wide):
    owners, rows, width = got_ref.shape
    body = rows - NOTE
    per_owner, rank_width, features = a_ref.shape
    for owner in range(owners):
        wide[owner * body : (owner + 1) * body, :] = got_ref[owner, :body, :].astype(jnp.float32)
    blocks = features // width
    total = seats * steps
    x = jnp.concatenate(
        [wide[pl.ds(c, total, stride=blocks), :].astype(jnp.bfloat16) for c in range(blocks)], axis=1
    )
    per_group = total // owners
    for owner in range(owners):
        slot_ref[owner * per_group : (owner + 1) * per_group, :] = got_ref[owner, body:, :].astype(
            jnp.float32
        )[:per_group]
    every = dot(x, a_ref[...].reshape(per_owner * rank_width, features), (1, 1))
    slot = slot_ref[...].astype(jnp.int32)
    lane = lax.broadcasted_iota(jnp.int32, (total, width), 1)
    per_block = width // rank_width
    kept = jnp.zeros((total, width), jnp.float32)
    for c in range(per_owner // per_block):
        mine = slot == c * per_block + lane // rank_width
        kept = kept + jnp.where(mine, every[:, c * width : (c + 1) * width], 0.0)
    folded = kept
    for k in range(1, per_block):
        folded = folded + pltpu.roll(kept, k * rank_width, 1)
    low_ref[...] = folded


def low(got, a_turned, seats, steps):
    owners, rows, width = got.shape
    total = seats * steps
    return pl.pallas_call(
        functools.partial(low_kernel, seats, steps),
        out_shape=[
            jax.ShapeDtypeStruct((total, width), jnp.float32),
            jax.ShapeDtypeStruct((total, width), jnp.float32),
        ],
        in_specs=[pl.BlockSpec(memory_space=pltpu.VMEM)] * 2,
        out_specs=[pl.BlockSpec(memory_space=pltpu.VMEM)] * 2,
        scratch_shapes=[pltpu.VMEM((owners * (rows - NOTE), width), jnp.float32)],
        compiler_params=pltpu.CompilerParams(vmem_limit_bytes=SMALL_VMEM),
        cost_estimate=pl.CostEstimate(
            flops=2 * total * a_turned.size, bytes_accessed=2 * a_turned.size, transcendentals=0
        ),
        name="low",
    )(got, a_turned)


def update_kernel(own_ref, other_ref, slot_ref, factor_ref, b_ref, back_ref, wide):
    total, width = own_ref.shape
    per_owner, rank_width, columns = b_ref.shape
    owners, body, _ = back_ref.shape
    summed = own_ref[...]
    for k in range(other_ref.shape[0]):
        summed = summed + other_ref[k]
    slot = slot_ref[...].astype(jnp.int32)
    lane = lax.broadcasted_iota(jnp.int32, (total, width), 1)
    per_block = width // rank_width
    spread = []
    for c in range(per_owner // per_block):
        mine = slot == c * per_block + lane // rank_width
        scaled = summed * factor_ref[:, c * width : (c + 1) * width]
        spread.append(jnp.where(mine, scaled, 0.0).astype(jnp.bfloat16))
    spread = jnp.concatenate(spread, axis=1)
    result = dot(spread, b_ref[...].reshape(per_owner * rank_width, columns))
    blocks = columns // width
    for c in range(blocks):
        wide[pl.ds(c, total, stride=blocks), :] = result[:, c * width : (c + 1) * width]
    for owner in range(owners):
        back_ref[owner] = wide[owner * body : (owner + 1) * body, :].astype(jnp.bfloat16)


def update(own, others, slot, factor, b_store, owners):
    total, width = own.shape
    columns = b_store.shape[2]
    body = total * columns // width // owners
    return pl.pallas_call(
        update_kernel,
        out_shape=jax.ShapeDtypeStruct((owners, body, width), jnp.bfloat16),
        in_specs=[pl.BlockSpec(memory_space=pltpu.VMEM)] * 5,
        out_specs=pl.BlockSpec(memory_space=pltpu.VMEM),
        scratch_shapes=[pltpu.VMEM((owners * body, width), jnp.float32)],
        compiler_params=pltpu.CompilerParams(vmem_limit_bytes=SMALL_VMEM),
        cost_estimate=pl.CostEstimate(
            flops=2 * total * b_store.size, bytes_accessed=2 * b_store.size, transcendentals=0
        ),
        name="update",
    )(own, others, slot, factor, b_store)


def finish_kernel(seat, core, back_ref, base_ref, other_ref, out_ref, wide):
    requests, steps, columns = out_ref.shape
    owners, body, width = back_ref.shape
    rows = body // QCAP
    blocks = columns // width
    total = requests * steps
    for request in range(requests):
        owner = seat[request] // QCAP
        turn = seat[request] % QCAP
        wide[request * rows : (request + 1) * rows, :] = back_ref[
            owner, pl.ds(pl.multiple_of(turn * rows, rows), rows), :
        ].astype(jnp.float32)
    for c in range(blocks):
        here = slice(c * width, (c + 1) * width)
        mixed = base_ref[:, here]
        for k in range(other_ref.shape[0]):
            mixed = mixed + other_ref[k, :, here].astype(jnp.float32)
        mixed = mixed + wide[pl.ds(c, total, stride=blocks), :]
        out_ref[:, :, here] = mixed.reshape(requests, steps, width).astype(out_ref.dtype)


def finish(seat, core, back, partial_out, others, requests, steps, columns):
    owners, body, width = back.shape
    total = requests * steps
    return pl.pallas_call(
        finish_kernel,
        grid_spec=pltpu.PrefetchScalarGridSpec(
            num_scalar_prefetch=2,
            grid=(1,),
            in_specs=[
                pl.BlockSpec(back.shape, lambda i, seat, core: (0, 0, 0)),
                pl.BlockSpec((total, columns), lambda i, seat, core: (0, core[0])),
                pl.BlockSpec(others.shape, lambda i, seat, core: (0, 0, 0)),
            ],
            out_specs=pl.BlockSpec((requests, steps, columns), lambda i, seat, core: (0, 0, 0)),
            scratch_shapes=[pltpu.VMEM((requests * body // QCAP, width), jnp.float32)],
        ),
        out_shape=jax.ShapeDtypeStruct((requests, steps, columns), jnp.bfloat16),
        compiler_params=pltpu.CompilerParams(vmem_limit_bytes=SMALL_VMEM),
        cost_estimate=pl.CostEstimate(
            flops=3 * total * columns, bytes_accessed=12 * total * columns, transcendentals=0
        ),
        name="finish",
    )(seat, core, back, partial_out, others)


def local(queries, kv_cache, new_kv, lengths, adapter_ids, place, ranks, w_out, a_store, b_store):
    request_count, step_count = (queries.shape[0], queries.shape[1])
    owners = lax.axis_size("store")
    cores = lax.axis_size("tensor")
    core = lax.axis_index("tensor")
    per_owner, feature_half, rank_width = a_store.shape
    out_half = b_store.shape[2]
    seats = owners * QCAP
    shifts = [[(k, (k + step) % cores) for k in range(cores)] for step in range(1, cores)]

    attended, sent, seat = attend(
        queries, kv_cache, new_kv, lengths, adapter_ids, place, owners, per_owner
    )
    got = lax.all_to_all(sent, "store", split_axis=0, concat_axis=0, tiled=True)

    partial_out = jnp.dot(
        attended.reshape(request_count * step_count, feature_half),
        w_out,
        preferred_element_type=jnp.float32,
    )
    here = lax.axis_index("store") * per_owner + jnp.arange(per_owner, dtype=jnp.int32)
    slot_rank = jnp.sum(jnp.where(here[:, None] == place[None, :], ranks[None, :], 0), axis=1)
    factor = rank_factor(slot_rank, rank_width).reshape(1, per_owner * rank_width)

    got, partial_out = lax.optimization_barrier((got, partial_out))
    own, slot = low(got, jnp.swapaxes(a_store, 1, 2), seats, step_count)
    others = jnp.stack([lax.ppermute(own, "tensor", shift) for shift in shifts])
    back = update(own, others, slot, factor, b_store, owners)
    back, partial_out = lax.optimization_barrier((back, partial_out))
    back = lax.all_to_all(back, "store", split_axis=0, concat_axis=0, tiled=True)

    shares = []
    for step, shift in enumerate(shifts, 1):
        target = (core + step) % cores
        share = lax.dynamic_slice_in_dim(partial_out, target * out_half, out_half, 1)
        shares.append(lax.ppermute(share, "tensor", shift))
    return finish(
        seat, core.reshape(1), back, partial_out, jnp.stack(shares), request_count, step_count, out_half
    )


def solution(mesh):
    return jax.shard_map(
        local,
        mesh=mesh,
        in_specs=(
            P(("rep", "store"), None, "tensor", None),
            P(None, ("rep", "store"), "tensor", None, None),
            P(None, ("rep", "store"), None, "tensor", None),
            P(("rep", "store")),
            P(("rep", "store")),
            P("rep"),
            P("rep"),
            P("tensor", None),
            P(("rep", "store"), "tensor", None),
            P(("rep", "store"), None, "tensor"),
        ),
        out_specs=P(("rep", "store"), None, "tensor"),
        check_vma=False,
    )
```

```python
import functools
import math

import jax
import jax.numpy as jnp
from jax import lax
from jax.experimental import pallas as pl
from jax.experimental.pallas import tpu as pltpu
from jax.sharding import PartitionSpec as P

QCAP = 3
LANES = 128
NOTE = 16
ATTEND_VMEM = 24 * 1024 * 1024
TILE = 1024
BASE_VMEM = 32 * 1024 * 1024
BATCH = 12
FINISH = 2
SMALL_VMEM = 16 * 1024 * 1024

adapter_scale = 8.0


def dot(left, right, contract=(1, 0)):
    return lax.dot_general(
        left, right, (((contract[0],), (contract[1],)), ((), ())), preferred_element_type=jnp.float32
    )


def far(x):
    return pltpu.with_memory_space_constraint(x, pltpu.HBM)


def near(x):
    return pltpu.with_memory_space_constraint(x, pltpu.VMEM)


def attend_kernel(
    steps, heads, per_owner,
    lengths, adapter_ids, place,
    q_ref, kv_ref, new_ref,
    attended_ref, sent_ref, seat_ref,
    taken, slots,
):
    owners = taken.shape[0]
    seats = owners * QCAP
    requests = seat_ref.shape[0]
    batch, rows, width = q_ref.shape
    slots_in_cache = kv_ref.shape[3]
    group = heads // 2
    step = pl.program_id(0)

    @pl.when(step == 0)
    def _():
        for owner in range(owners):
            taken[owner] = 0
        for seat in range(seats):
            slots[seat] = 0
        if seats > requests:
            sent_ref[...] = jnp.zeros_like(sent_ref)

    row = lax.broadcasted_iota(jnp.int32, (rows, width), 0)
    first = (row // group) % 2 == 0
    new_count = new_ref.shape[2]
    new_row = lax.broadcasted_iota(jnp.int32, (rows, new_count), 0)
    new_column = lax.broadcasted_iota(jnp.int32, (rows, new_count), 1)
    new_seen = (new_column // 2 <= new_row // heads) & (new_column % 2 == (new_row // group) % 2)
    column = lax.broadcasted_iota(jnp.int32, (rows, slots_in_cache), 1)
    scale = 1.0 / math.sqrt(width)

    cached, fresh = [], []
    for j in range(batch):
        q = q_ref[j]
        q_wide = q.astype(jnp.float32)
        both = jnp.concatenate(
            [jnp.where(first, q_wide, 0.0), jnp.where(first, 0.0, q_wide)], axis=1
        ).astype(jnp.bfloat16)
        keys = jnp.concatenate([kv_ref[0, j, 0], kv_ref[0, j, 1]], axis=1)
        scores = dot(both, keys, (1, 1)) * scale
        cached.append(jnp.where(column < lengths[step * batch + j], scores, -jnp.inf))
        scores = dot(q, new_ref[0, j], (1, 1)) * scale
        fresh.append(jnp.where(new_seen, scores, -jnp.inf))
    tops = [
        jnp.maximum(jnp.max(a, axis=1, keepdims=True), jnp.max(b, axis=1, keepdims=True))
        for a, b in zip(cached, fresh)
    ]
    cached = [jnp.exp(a - top) for a, top in zip(cached, tops)]
    fresh = [jnp.exp(b - top) for b, top in zip(fresh, tops)]
    sums = [
        1.0 / (jnp.sum(a, axis=1, keepdims=True) + jnp.sum(b, axis=1, keepdims=True))
        for a, b in zip(cached, fresh)
    ]
    cached = [(a * inv).astype(jnp.bfloat16) for a, inv in zip(cached, sums)]
    fresh = [(b * inv).astype(jnp.bfloat16) for b, inv in zip(fresh, sums)]
    for j in range(batch):
        values = jnp.concatenate([kv_ref[1, j, 0], kv_ref[1, j, 1]], axis=1)
        both = dot(cached[j], values)
        result = jnp.where(first, both[:, :width], both[:, width:]) + dot(fresh[j], new_ref[1, j])
        result = result.astype(jnp.bfloat16)
        request = step * batch + j
        location = place[adapter_ids[request]]
        owner = location // per_owner
        turn = taken[owner]
        taken[owner] = turn + 1
        slots[owner * QCAP + turn] = location % per_owner
        seat_ref[request] = owner * QCAP + turn
        attended_ref[request] = result
        sent_ref[owner, pl.ds(pl.multiple_of(turn * rows, rows), rows), :] = result

    @pl.when(step == steps - 1)
    def _():
        note_row = lax.broadcasted_iota(jnp.int32, (NOTE, width), 0)
        per_seat = rows // heads
        for owner in range(owners):
            note = jnp.zeros((NOTE, width), jnp.int32)
            for turn in range(QCAP):
                note = jnp.where(note_row // per_seat == turn, slots[owner * QCAP + turn], note)
            sent_ref[owner, QCAP * rows :, :] = note.astype(jnp.float32).astype(jnp.bfloat16)


def attend(queries, kv_cache, new_kv, lengths, adapter_ids, place, owners, per_owner):
    requests, step_count, heads, width = queries.shape
    cache_slots = kv_cache.shape[3]
    rows = step_count * heads
    new_rows = new_kv.shape[2] * new_kv.shape[3]
    batch = BATCH if requests % BATCH == 0 else 1
    steps = requests // batch
    body = QCAP * rows + NOTE
    return pl.pallas_call(
        functools.partial(attend_kernel, steps, heads, per_owner),
        grid_spec=pltpu.PrefetchScalarGridSpec(
            num_scalar_prefetch=3,
            grid=(steps,),
            in_specs=[
                pl.BlockSpec((batch, rows, width), lambda i, *_: (i, 0, 0)),
                pl.BlockSpec((2, batch, 2, cache_slots, width), lambda i, *_: (0, i, 0, 0, 0)),
                pl.BlockSpec((2, batch, new_rows, width), lambda i, *_: (0, i, 0, 0)),
            ],
            out_specs=[
                pl.BlockSpec(memory_space=pltpu.VMEM),
                pl.BlockSpec((owners, body, width), lambda i, *_: (0, 0, 0)),
                pl.BlockSpec(memory_space=pltpu.SMEM),
            ],
            scratch_shapes=[
                pltpu.SMEM((owners,), jnp.int32),
                pltpu.SMEM((owners * QCAP,), jnp.int32),
            ],
        ),
        out_shape=[
            pltpu.VMEM((requests, rows, width), jnp.bfloat16),
            pltpu.HBM((owners, body, width), jnp.bfloat16),
            jax.ShapeDtypeStruct((requests,), jnp.int32),
        ],
        compiler_params=pltpu.CompilerParams(
            dimension_semantics=("arbitrary",), vmem_limit_bytes=ATTEND_VMEM
        ),
        cost_estimate=pl.CostEstimate(
            flops=4 * requests * rows * cache_slots * width * 2,
            bytes_accessed=kv_cache.size * 2 + 4 * queries.size,
            transcendentals=requests * rows * cache_slots,
        ),
        name="attend",
    )(
        far(lengths),
        far(adapter_ids),
        far(place),
        far(queries.reshape(requests, rows, width)),
        far(kv_cache),
        far(new_kv.reshape(2, requests, new_rows, width)),
    )


def other_columns_kernel(
    block, here, place, ranks,
    attended_ref, w_ref, a_ref,
    out_ref, x_ref, a_near, factor_ref,
    wide, arrived,
):
    copy = pltpu.make_async_copy(a_ref, a_near, arrived)
    last = pl.program_id(0) == pl.num_programs(0) - 1

    @pl.when(pl.program_id(0) == 0)
    def _():
        total, width = x_ref.shape[0], wide.shape[1]
        blocks = x_ref.shape[1] // width
        wide[...] = attended_ref[...].reshape(wide.shape).astype(jnp.float32)
        for c in range(blocks):
            x_ref[:, c * width : (c + 1) * width] = wide[pl.ds(c, total, stride=blocks), :].astype(
                jnp.bfloat16
            )

    @pl.when(last)
    def _():
        copy.start()

    out_ref[...] = dot(x_ref[...], w_ref[...])

    @pl.when(last)
    def _():
        rank_width = a_ref.shape[1]
        part = lax.broadcasted_iota(jnp.int32, factor_ref.shape, 0)
        lane = lax.broadcasted_iota(jnp.int32, factor_ref.shape, 1)
        position = here[0] + (part * factor_ref.shape[1] + lane) // rank_width
        rank = jnp.zeros(factor_ref.shape, jnp.int32)
        for adapter in range(place.shape[0]):
            rank = rank + jnp.where(position == place[adapter], ranks[adapter], 0)
        scale = adapter_scale / jnp.sqrt(rank.astype(jnp.float32))
        factor_ref[...] = jnp.where(lane % rank_width < rank, scale, 0.0)
        copy.wait()


def other_columns(attended, w_out, block, columns, here, place, ranks, a_turned):
    requests, rows, width = attended.shape
    features = w_out.shape[0]
    total = requests * rows * width // features
    tile = min(TILE, columns)
    steps = columns // tile
    parts = a_turned.shape[0] * a_turned.shape[1] // width
    whole = pl.BlockSpec(memory_space=pltpu.VMEM)
    return pl.pallas_call(
        other_columns_kernel,
        grid_spec=pltpu.PrefetchScalarGridSpec(
            num_scalar_prefetch=4,
            grid=(steps,),
            in_specs=[
                whole,
                pl.BlockSpec((features, tile), lambda i, block, *_: (0, block[0] * steps + i)),
                pl.BlockSpec(memory_space=pl.ANY),
            ],
            out_specs=[
                pl.BlockSpec((total, tile), lambda i, *_: (0, i)),
                pl.BlockSpec((total, features), lambda i, *_: (0, 0)),
                whole,
                whole,
            ],
            scratch_shapes=[
                pltpu.VMEM((requests * rows, width), jnp.float32),
                pltpu.SemaphoreType.DMA,
            ],
        ),
        out_shape=[
            jax.ShapeDtypeStruct((total, columns), jnp.float32),
            pltpu.HBM((total, features), jnp.bfloat16),
            pltpu.VMEM(a_turned.shape, a_turned.dtype),
            pltpu.VMEM((parts, width), jnp.float32),
        ],
        compiler_params=pltpu.CompilerParams(
            dimension_semantics=("arbitrary",), vmem_limit_bytes=BASE_VMEM
        ),
        cost_estimate=pl.CostEstimate(
            flops=2 * total * features * columns,
            bytes_accessed=2 * features * columns + 4 * a_turned.size,
            transcendentals=0,
        ),
        name="other_columns",
    )(block, here, far(place), far(ranks), near(attended), far(w_out), far(a_turned))


def own_columns_kernel(block, x_ref, w_ref, share_ref, out_ref):
    out_ref[...] = dot(x_ref[...], w_ref[...]) + share_ref[...]


def own_columns(x, w_out, block, columns, share):
    total, features = x.shape
    tile = min(TILE, columns)
    steps = columns // tile
    return pl.pallas_call(
        own_columns_kernel,
        grid_spec=pltpu.PrefetchScalarGridSpec(
            num_scalar_prefetch=1,
            grid=(steps,),
            in_specs=[
                pl.BlockSpec((total, features), lambda i, block: (0, 0)),
                pl.BlockSpec((features, tile), lambda i, block: (0, block[0] * steps + i)),
                pl.BlockSpec((total, tile), lambda i, block: (0, i)),
            ],
            out_specs=pl.BlockSpec((total, tile), lambda i, block: (0, i)),
        ),
        out_shape=jax.ShapeDtypeStruct((total, columns), jnp.float32),
        compiler_params=pltpu.CompilerParams(
            dimension_semantics=("arbitrary",), vmem_limit_bytes=BASE_VMEM
        ),
        cost_estimate=pl.CostEstimate(
            flops=2 * total * features * columns, bytes_accessed=2 * features * columns, transcendentals=0
        ),
        name="own_columns",
    )(block, far(x), far(w_out), share)


def low_kernel(seats, steps, got_ref, a_ref, low_ref, slot_ref, wide):
    owners, rows, width = got_ref.shape
    body = rows - NOTE
    per_owner, rank_width, features = a_ref.shape
    for owner in range(owners):
        wide[owner * body : (owner + 1) * body, :] = got_ref[owner, :body, :].astype(jnp.float32)
    blocks = features // width
    total = seats * steps
    x = jnp.concatenate(
        [wide[pl.ds(c, total, stride=blocks), :].astype(jnp.bfloat16) for c in range(blocks)], axis=1
    )
    per_group = total // owners
    for owner in range(owners):
        slot_ref[owner * per_group : (owner + 1) * per_group, :] = got_ref[owner, body:, :].astype(
            jnp.float32
        )[:per_group]
    every = dot(x, a_ref[...].reshape(per_owner * rank_width, features), (1, 1))
    slot = slot_ref[...].astype(jnp.int32)
    lane = lax.broadcasted_iota(jnp.int32, (total, width), 1)
    per_block = width // rank_width
    kept = jnp.zeros((total, width), jnp.float32)
    for c in range(per_owner // per_block):
        mine = slot == c * per_block + lane // rank_width
        kept = kept + jnp.where(mine, every[:, c * width : (c + 1) * width], 0.0)
    folded = kept
    for k in range(1, per_block):
        folded = folded + pltpu.roll(kept, k * rank_width, 1)
    low_ref[...] = folded


def low(got, a_turned, seats, steps):
    owners, rows, width = got.shape
    total = seats * steps
    return pl.pallas_call(
        functools.partial(low_kernel, seats, steps),
        out_shape=[
            jax.ShapeDtypeStruct((total, width), jnp.float32),
            jax.ShapeDtypeStruct((total, width), jnp.float32),
        ],
        in_specs=[pl.BlockSpec(memory_space=pltpu.VMEM)] * 2,
        out_specs=[pl.BlockSpec(memory_space=pltpu.VMEM)] * 2,
        scratch_shapes=[pltpu.VMEM((owners * (rows - NOTE), width), jnp.float32)],
        compiler_params=pltpu.CompilerParams(vmem_limit_bytes=SMALL_VMEM),
        cost_estimate=pl.CostEstimate(
            flops=2 * total * a_turned.size, bytes_accessed=2 * a_turned.size, transcendentals=0
        ),
        name="low",
    )(got, near(a_turned))


def update_kernel(own_ref, other_ref, slot_ref, factor_ref, b_ref, back_ref, wide, ready, left):
    total, width = own_ref.shape
    per_owner, rank_width, columns = b_ref.shape
    owners, body, _ = back_ref.shape
    per_block = width // rank_width
    blocks = columns // width
    parts = per_owner // per_block
    summed = own_ref[...]
    for k in range(other_ref.shape[0]):
        summed = summed + other_ref[k]
    slot = slot_ref[...].astype(jnp.int32)
    lane = lax.broadcasted_iota(jnp.int32, (total, width), 1)
    spread = []
    for c in range(parts):
        mine = slot == c * per_block + lane // rank_width
        scaled = summed * factor_ref[c : c + 1, :]
        spread.append(jnp.where(mine, scaled, 0.0).astype(jnp.bfloat16))
    spread = jnp.concatenate(spread, axis=1)
    result = dot(spread, b_ref[...].reshape(per_owner * rank_width, columns))
    for c in range(blocks):
        wide[pl.ds(c, total, stride=blocks), :] = result[:, c * width : (c + 1) * width]
    half = owners // 2
    leaving = []
    for start, end in ((0, half), (half, owners)):
        for owner in range(start, end):
            ready[owner] = wide[owner * body : (owner + 1) * body, :].astype(jnp.bfloat16)
        few = pl.ds(start, end - start)
        leaving.append(pltpu.make_async_copy(ready.at[few], back_ref.at[few], left.at[len(leaving)]))
        leaving[-1].start()
    for copy in leaving:
        copy.wait()


def update(own, others, slot, factor, b_store, owners):
    total, width = own.shape
    columns = b_store.shape[2]
    body = total * columns // width // owners
    return pl.pallas_call(
        update_kernel,
        out_shape=pltpu.HBM((owners, body, width), jnp.bfloat16),
        in_specs=[pl.BlockSpec(memory_space=pltpu.VMEM)] * 5,
        out_specs=pl.BlockSpec(memory_space=pl.ANY),
        scratch_shapes=[
            pltpu.VMEM((owners * body, width), jnp.float32),
            pltpu.VMEM((owners, body, width), jnp.bfloat16),
            pltpu.SemaphoreType.DMA((2,)),
        ],
        compiler_params=pltpu.CompilerParams(vmem_limit_bytes=SMALL_VMEM),
        cost_estimate=pl.CostEstimate(
            flops=2 * total * b_store.size, bytes_accessed=2 * b_store.size, transcendentals=0
        ),
        name="update",
    )(own, others, slot, near(factor), near(b_store))


def finish_kernel(parts, seat, back_ref, base_ref, out_ref, wide, ready, left):
    requests, steps, columns = out_ref.shape
    owners, body, width = back_ref.shape
    rows = body // QCAP
    blocks = columns // width
    few = requests // parts
    total = few * steps
    leaving = []
    for part in range(parts):
        for request in range(part * few, (part + 1) * few):
            owner, turn = seat[request] // QCAP, seat[request] % QCAP
            wide[request * rows : (request + 1) * rows, :] = back_ref[
                owner, pl.ds(pl.multiple_of(turn * rows, rows), rows), :
            ].astype(jnp.float32)
        mine = pl.ds(part * few, few)
        for c in range(blocks):
            here = slice(c * width, (c + 1) * width)
            mixed = base_ref[part * total : (part + 1) * total, here]
            mixed = mixed + wide[pl.ds(part * few * rows + c, total, stride=blocks), :]
            ready[mine, :, here] = mixed.reshape(few, steps, width).astype(ready.dtype)
        leaving.append(pltpu.make_async_copy(ready.at[mine], out_ref.at[mine], left.at[part]))
        leaving[-1].start()
    for copy in leaving:
        copy.wait()


def finish(seat, back, base, requests, steps):
    owners, body, width = back.shape
    total, columns = base.shape
    parts = FINISH if requests % FINISH == 0 else 1
    return pl.pallas_call(
        functools.partial(finish_kernel, parts),
        in_specs=[
            pl.BlockSpec(memory_space=pltpu.SMEM),
            pl.BlockSpec(memory_space=pltpu.VMEM),
            pl.BlockSpec(memory_space=pltpu.VMEM),
        ],
        out_specs=pl.BlockSpec(memory_space=pl.ANY),
        scratch_shapes=[
            pltpu.VMEM((requests * body // QCAP, width), jnp.float32),
            pltpu.VMEM((requests, steps, columns), jnp.bfloat16),
            pltpu.SemaphoreType.DMA((parts,)),
        ],
        out_shape=jax.ShapeDtypeStruct((requests, steps, columns), jnp.bfloat16),
        compiler_params=pltpu.CompilerParams(vmem_limit_bytes=SMALL_VMEM),
        cost_estimate=pl.CostEstimate(
            flops=2 * total * columns, bytes_accessed=8 * total * columns, transcendentals=0
        ),
        name="finish",
    )(seat, back, base)


def local(queries, kv_cache, new_kv, lengths, adapter_ids, place, ranks, w_out, a_store, b_store):
    request_count, step_count = (queries.shape[0], queries.shape[1])
    owners = lax.axis_size("store")
    cores = lax.axis_size("tensor")
    core = lax.axis_index("tensor")
    per_owner, feature_half, rank_width = a_store.shape
    out_half = b_store.shape[2]
    seats = owners * QCAP
    shifts = [[(k, (k + step) % cores) for k in range(cores)] for step in range(1, cores)]

    attended, sent, seat = attend(
        queries, kv_cache, new_kv, lengths, adapter_ids, place, owners, per_owner
    )
    got = lax.all_to_all(sent, "store", split_axis=0, concat_axis=0, tiled=True)

    blocks = [((core + step) % cores).reshape(1) for step in range(cores)]
    a_turned = jnp.swapaxes(a_store, 1, 2)
    here = (lax.axis_index("store") * per_owner).reshape(1)
    share, x, a_near, factor = other_columns(
        attended, w_out, blocks[1], out_half, here, place, ranks, a_turned
    )
    share = lax.ppermute(share, "tensor", shifts[0])

    own, slot = low(got, a_near, seats, step_count)
    others = jnp.stack([lax.ppermute(own, "tensor", shift) for shift in shifts])
    back = update(own, others, slot, factor, b_store, owners)
    back, x, share = lax.optimization_barrier((back, x, share))
    back = lax.all_to_all(back, "store", split_axis=0, concat_axis=0, tiled=True)
    for step in range(2, cores):
        more = own_columns(x, w_out, blocks[step], out_half, jnp.zeros_like(share))
        share = share + lax.ppermute(more, "tensor", shifts[step - 1])
    base = own_columns(x, w_out, blocks[0], out_half, share)
    return finish(seat, back, base, request_count, step_count)


def solution(mesh):
    return jax.shard_map(
        local,
        mesh=mesh,
        in_specs=(
            P(("rep", "store"), None, "tensor", None),
            P(None, ("rep", "store"), "tensor", None, None),
            P(None, ("rep", "store"), None, "tensor", None),
            P(("rep", "store")),
            P(("rep", "store")),
            P("rep"),
            P("rep"),
            P("tensor", None),
            P(("rep", "store"), "tensor", None),
            P(("rep", "store"), None, "tensor"),
        ),
        out_specs=P(("rep", "store"), None, "tensor"),
        check_vma=False,
    )
```

```python
import functools
import math

import jax
import jax.numpy as jnp
from jax import lax
from jax.experimental import pallas as pl
from jax.experimental.pallas import tpu as pltpu
from jax.sharding import PartitionSpec as P

QCAP = 3
LANES = 128
NOTE = 16
ATTEND_VMEM = 24 * 1024 * 1024
TILE = 1024
BASE_VMEM = 32 * 1024 * 1024
FINISH = 2
SMALL_VMEM = 16 * 1024 * 1024

adapter_scale = 8.0


def dot(left, right, contract=(1, 0)):
    return lax.dot_general(
        left, right, (((contract[0],), (contract[1],)), ((), ())), preferred_element_type=jnp.float32
    )


def far(x):
    return pltpu.with_memory_space_constraint(x, pltpu.HBM)


def near(x):
    return pltpu.with_memory_space_constraint(x, pltpu.VMEM)


def attend_kernel(
    sizes, heads, per_owner,
    lengths, adapter_ids, place,
    q_far, kv_far, new_far,
    attended_ref, sent_ref, seat_ref,
    q_ref, kv_ref, new_ref, taken, slots, arrived,
):
    owners = taken.shape[0]
    requests, rows, width = attended_ref.shape
    slots_in_cache = kv_ref.shape[3]
    group = heads // 2
    coming = [
        pltpu.make_async_copy(q_far, q_ref, arrived.at[0]),
        pltpu.make_async_copy(new_far, new_ref, arrived.at[1]),
    ]
    end = 0
    for size in sizes:
        few = pl.ds(end, size)
        end = end + size
        coming.append(
            pltpu.make_async_copy(kv_far.at[:, few], kv_ref.at[:, few], arrived.at[len(coming)])
        )
    for copy in coming:
        copy.start()

    for owner in range(owners):
        taken[owner] = 0
    for seat in range(owners * QCAP):
        slots[seat] = 0
    if owners * QCAP > requests:
        sent_ref[...] = jnp.zeros_like(sent_ref)

    row = lax.broadcasted_iota(jnp.int32, (rows, width), 0)
    first = (row // group) % 2 == 0
    new_count = new_ref.shape[2]
    new_row = lax.broadcasted_iota(jnp.int32, (rows, new_count), 0)
    new_column = lax.broadcasted_iota(jnp.int32, (rows, new_count), 1)
    new_seen = (new_column // 2 <= new_row // heads) & (new_column % 2 == (new_row // group) % 2)
    column = lax.broadcasted_iota(jnp.int32, (rows, slots_in_cache), 1)
    scale = 1.0 / math.sqrt(width)

    coming[0].wait()
    coming[1].wait()
    end = 0
    for size, copy in zip(sizes, coming[2:]):
        start, end = end, end + size
        copy.wait()
        cached, fresh = [], []
        for r in range(start, end):
            q = q_ref[r]
            q_wide = q.astype(jnp.float32)
            both = jnp.concatenate(
                [jnp.where(first, q_wide, 0.0), jnp.where(first, 0.0, q_wide)], axis=1
            ).astype(jnp.bfloat16)
            keys = jnp.concatenate([kv_ref[0, r, 0], kv_ref[0, r, 1]], axis=1)
            scores = dot(both, keys, (1, 1)) * scale
            cached.append(jnp.where(column < lengths[r], scores, -jnp.inf))
            scores = dot(q, new_ref[0, r], (1, 1)) * scale
            fresh.append(jnp.where(new_seen, scores, -jnp.inf))
        tops = [
            jnp.maximum(jnp.max(a, axis=1, keepdims=True), jnp.max(b, axis=1, keepdims=True))
            for a, b in zip(cached, fresh)
        ]
        cached = [jnp.exp(a - top) for a, top in zip(cached, tops)]
        fresh = [jnp.exp(b - top) for b, top in zip(fresh, tops)]
        sums = [
            1.0 / (jnp.sum(a, axis=1, keepdims=True) + jnp.sum(b, axis=1, keepdims=True))
            for a, b in zip(cached, fresh)
        ]
        cached = [(a * inv).astype(jnp.bfloat16) for a, inv in zip(cached, sums)]
        fresh = [(b * inv).astype(jnp.bfloat16) for b, inv in zip(fresh, sums)]
        for a, b, r in zip(cached, fresh, range(start, end)):
            values = jnp.concatenate([kv_ref[1, r, 0], kv_ref[1, r, 1]], axis=1)
            both = dot(a, values)
            result = jnp.where(first, both[:, :width], both[:, width:]) + dot(b, new_ref[1, r])
            result = result.astype(jnp.bfloat16)
            location = place[adapter_ids[r]]
            owner = location // per_owner
            turn = taken[owner]
            taken[owner] = turn + 1
            slots[owner * QCAP + turn] = location % per_owner
            seat_ref[r] = owner * QCAP + turn
            attended_ref[r] = result
            sent_ref[owner, pl.ds(pl.multiple_of(turn * rows, rows), rows), :] = result

    note_row = lax.broadcasted_iota(jnp.int32, (NOTE, width), 0)
    per_seat = rows // heads
    for owner in range(owners):
        note = jnp.zeros((NOTE, width), jnp.int32)
        for turn in range(QCAP):
            note = jnp.where(note_row // per_seat == turn, slots[owner * QCAP + turn], note)
        sent_ref[owner, QCAP * rows :, :] = note.astype(jnp.float32).astype(jnp.bfloat16)


def attend(queries, kv_cache, new_kv, lengths, adapter_ids, place, owners, per_owner):
    requests, step_count, heads, width = queries.shape
    rows = step_count * heads
    new_rows = new_kv.shape[2] * new_kv.shape[3]
    body = QCAP * rows + NOTE
    sizes = [requests // 6, requests // 3]
    sizes = [size for size in [*sizes, requests - sum(sizes)] if size]
    queries = queries.reshape(requests, rows, width)
    new_kv = new_kv.reshape(2, requests, new_rows, width)
    anywhere = pl.BlockSpec(memory_space=pl.ANY)
    return pl.pallas_call(
        functools.partial(attend_kernel, sizes, heads, per_owner),
        grid_spec=pltpu.PrefetchScalarGridSpec(
            num_scalar_prefetch=3,
            grid=(1,),
            in_specs=[anywhere, anywhere, anywhere],
            out_specs=[
                pl.BlockSpec(memory_space=pltpu.VMEM),
                pl.BlockSpec((owners, body, width), lambda i, *_: (0, 0, 0)),
                pl.BlockSpec(memory_space=pltpu.SMEM),
            ],
            scratch_shapes=[
                pltpu.VMEM(queries.shape, queries.dtype),
                pltpu.VMEM(kv_cache.shape, kv_cache.dtype),
                pltpu.VMEM(new_kv.shape, new_kv.dtype),
                pltpu.SMEM((owners,), jnp.int32),
                pltpu.SMEM((owners * QCAP,), jnp.int32),
                pltpu.SemaphoreType.DMA((2 + len(sizes),)),
            ],
        ),
        out_shape=[
            pltpu.VMEM((requests, rows, width), jnp.bfloat16),
            pltpu.HBM((owners, body, width), jnp.bfloat16),
            jax.ShapeDtypeStruct((requests,), jnp.int32),
        ],
        compiler_params=pltpu.CompilerParams(
            dimension_semantics=("arbitrary",), vmem_limit_bytes=ATTEND_VMEM
        ),
        cost_estimate=pl.CostEstimate(
            flops=4 * requests * rows * kv_cache.shape[3] * width * 2,
            bytes_accessed=kv_cache.size * 2 + 4 * queries.size,
            transcendentals=requests * rows * kv_cache.shape[3],
        ),
        name="attend",
    )(far(lengths), far(adapter_ids), far(place), far(queries), far(kv_cache), far(new_kv))


def other_columns_kernel(
    block, here, place, ranks,
    attended_ref, w_ref, a_ref,
    out_ref, x_ref, a_near, factor_ref,
    wide, arrived,
):
    copy = pltpu.make_async_copy(a_ref, a_near, arrived)
    last = pl.program_id(0) == pl.num_programs(0) - 1

    @pl.when(pl.program_id(0) == 0)
    def _():
        total, width = x_ref.shape[0], wide.shape[1]
        blocks = x_ref.shape[1] // width
        wide[...] = attended_ref[...].reshape(wide.shape).astype(jnp.float32)
        for c in range(blocks):
            x_ref[:, c * width : (c + 1) * width] = wide[pl.ds(c, total, stride=blocks), :].astype(
                jnp.bfloat16
            )

    @pl.when(last)
    def _():
        copy.start()

    out_ref[...] = dot(x_ref[...], w_ref[...])

    @pl.when(last)
    def _():
        rank_width = a_ref.shape[1]
        part = lax.broadcasted_iota(jnp.int32, factor_ref.shape, 0)
        lane = lax.broadcasted_iota(jnp.int32, factor_ref.shape, 1)
        position = here[0] + (part * factor_ref.shape[1] + lane) // rank_width
        rank = jnp.zeros(factor_ref.shape, jnp.int32)
        for adapter in range(place.shape[0]):
            rank = rank + jnp.where(position == place[adapter], ranks[adapter], 0)
        scale = adapter_scale / jnp.sqrt(rank.astype(jnp.float32))
        factor_ref[...] = jnp.where(lane % rank_width < rank, scale, 0.0)
        copy.wait()


def other_columns(attended, w_out, block, columns, here, place, ranks, a_turned):
    requests, rows, width = attended.shape
    features = w_out.shape[0]
    total = requests * rows * width // features
    tile = min(TILE, columns)
    steps = columns // tile
    parts = a_turned.shape[0] * a_turned.shape[1] // width
    whole = pl.BlockSpec(memory_space=pltpu.VMEM)
    return pl.pallas_call(
        other_columns_kernel,
        grid_spec=pltpu.PrefetchScalarGridSpec(
            num_scalar_prefetch=4,
            grid=(steps,),
            in_specs=[
                whole,
                pl.BlockSpec((features, tile), lambda i, block, *_: (0, block[0] * steps + i)),
                pl.BlockSpec(memory_space=pl.ANY),
            ],
            out_specs=[
                pl.BlockSpec((total, tile), lambda i, *_: (0, i)),
                pl.BlockSpec((total, features), lambda i, *_: (0, 0)),
                whole,
                whole,
            ],
            scratch_shapes=[
                pltpu.VMEM((requests * rows, width), jnp.float32),
                pltpu.SemaphoreType.DMA,
            ],
        ),
        out_shape=[
            jax.ShapeDtypeStruct((total, columns), jnp.float32),
            pltpu.HBM((total, features), jnp.bfloat16),
            pltpu.VMEM(a_turned.shape, a_turned.dtype),
            pltpu.VMEM((parts, width), jnp.float32),
        ],
        compiler_params=pltpu.CompilerParams(
            dimension_semantics=("arbitrary",), vmem_limit_bytes=BASE_VMEM
        ),
        cost_estimate=pl.CostEstimate(
            flops=2 * total * features * columns,
            bytes_accessed=2 * features * columns + 4 * a_turned.size,
            transcendentals=0,
        ),
        name="other_columns",
    )(block, here, far(place), far(ranks), near(attended), far(w_out), far(a_turned))


def own_columns_kernel(block, x_ref, w_ref, share_ref, out_ref):
    out_ref[...] = dot(x_ref[...], w_ref[...]) + share_ref[...]


def own_columns(x, w_out, block, columns, share):
    total, features = x.shape
    tile = min(TILE, columns)
    steps = columns // tile
    return pl.pallas_call(
        own_columns_kernel,
        grid_spec=pltpu.PrefetchScalarGridSpec(
            num_scalar_prefetch=1,
            grid=(steps,),
            in_specs=[
                pl.BlockSpec((total, features), lambda i, block: (0, 0)),
                pl.BlockSpec((features, tile), lambda i, block: (0, block[0] * steps + i)),
                pl.BlockSpec((total, tile), lambda i, block: (0, i)),
            ],
            out_specs=pl.BlockSpec((total, tile), lambda i, block: (0, i)),
        ),
        out_shape=jax.ShapeDtypeStruct((total, columns), jnp.float32),
        compiler_params=pltpu.CompilerParams(
            dimension_semantics=("arbitrary",), vmem_limit_bytes=BASE_VMEM
        ),
        cost_estimate=pl.CostEstimate(
            flops=2 * total * features * columns, bytes_accessed=2 * features * columns, transcendentals=0
        ),
        name="own_columns",
    )(block, far(x), far(w_out), share)


def low_kernel(seats, steps, got_ref, a_ref, low_ref, slot_ref, wide):
    owners, rows, width = got_ref.shape
    body = rows - NOTE
    per_owner, rank_width, features = a_ref.shape
    for owner in range(owners):
        wide[owner * body : (owner + 1) * body, :] = got_ref[owner, :body, :].astype(jnp.float32)
    blocks = features // width
    total = seats * steps
    x = jnp.concatenate(
        [wide[pl.ds(c, total, stride=blocks), :].astype(jnp.bfloat16) for c in range(blocks)], axis=1
    )
    per_group = total // owners
    for owner in range(owners):
        slot_ref[owner * per_group : (owner + 1) * per_group, :] = got_ref[owner, body:, :].astype(
            jnp.float32
        )[:per_group]
    every = dot(x, a_ref[...].reshape(per_owner * rank_width, features), (1, 1))
    slot = slot_ref[...].astype(jnp.int32)
    lane = lax.broadcasted_iota(jnp.int32, (total, width), 1)
    per_block = width // rank_width
    kept = jnp.zeros((total, width), jnp.float32)
    for c in range(per_owner // per_block):
        mine = slot == c * per_block + lane // rank_width
        kept = kept + jnp.where(mine, every[:, c * width : (c + 1) * width], 0.0)
    folded = kept
    for k in range(1, per_block):
        folded = folded + pltpu.roll(kept, k * rank_width, 1)
    low_ref[...] = folded


def low(got, a_turned, seats, steps):
    owners, rows, width = got.shape
    total = seats * steps
    return pl.pallas_call(
        functools.partial(low_kernel, seats, steps),
        out_shape=[
            jax.ShapeDtypeStruct((total, width), jnp.float32),
            jax.ShapeDtypeStruct((total, width), jnp.float32),
        ],
        in_specs=[pl.BlockSpec(memory_space=pltpu.VMEM)] * 2,
        out_specs=[pl.BlockSpec(memory_space=pltpu.VMEM)] * 2,
        scratch_shapes=[pltpu.VMEM((owners * (rows - NOTE), width), jnp.float32)],
        compiler_params=pltpu.CompilerParams(vmem_limit_bytes=SMALL_VMEM),
        cost_estimate=pl.CostEstimate(
            flops=2 * total * a_turned.size, bytes_accessed=2 * a_turned.size, transcendentals=0
        ),
        name="low",
    )(got, near(a_turned))


def update_kernel(own_ref, other_ref, slot_ref, factor_ref, b_ref, back_ref, wide, ready, left):
    total, width = own_ref.shape
    per_owner, rank_width, columns = b_ref.shape
    owners, body, _ = back_ref.shape
    per_block = width // rank_width
    blocks = columns // width
    parts = per_owner // per_block
    summed = own_ref[...]
    for k in range(other_ref.shape[0]):
        summed = summed + other_ref[k]
    slot = slot_ref[...].astype(jnp.int32)
    lane = lax.broadcasted_iota(jnp.int32, (total, width), 1)
    spread = []
    for c in range(parts):
        mine = slot == c * per_block + lane // rank_width
        scaled = summed * factor_ref[c : c + 1, :]
        spread.append(jnp.where(mine, scaled, 0.0).astype(jnp.bfloat16))
    spread = jnp.concatenate(spread, axis=1)
    result = dot(spread, b_ref[...].reshape(per_owner * rank_width, columns))
    for c in range(blocks):
        wide[pl.ds(c, total, stride=blocks), :] = result[:, c * width : (c + 1) * width]
    half = owners // 2
    leaving = []
    for start, end in ((0, half), (half, owners)):
        for owner in range(start, end):
            ready[owner] = wide[owner * body : (owner + 1) * body, :].astype(jnp.bfloat16)
        few = pl.ds(start, end - start)
        leaving.append(pltpu.make_async_copy(ready.at[few], back_ref.at[few], left.at[len(leaving)]))
        leaving[-1].start()
    for copy in leaving:
        copy.wait()


def update(own, others, slot, factor, b_store, owners):
    total, width = own.shape
    columns = b_store.shape[2]
    body = total * columns // width // owners
    return pl.pallas_call(
        update_kernel,
        out_shape=pltpu.HBM((owners, body, width), jnp.bfloat16),
        in_specs=[pl.BlockSpec(memory_space=pltpu.VMEM)] * 5,
        out_specs=pl.BlockSpec(memory_space=pl.ANY),
        scratch_shapes=[
            pltpu.VMEM((owners * body, width), jnp.float32),
            pltpu.VMEM((owners, body, width), jnp.bfloat16),
            pltpu.SemaphoreType.DMA((2,)),
        ],
        compiler_params=pltpu.CompilerParams(vmem_limit_bytes=SMALL_VMEM),
        cost_estimate=pl.CostEstimate(
            flops=2 * total * b_store.size, bytes_accessed=2 * b_store.size, transcendentals=0
        ),
        name="update",
    )(own, others, slot, near(factor), near(b_store))


def finish_kernel(parts, seat, back_ref, base_ref, out_ref, wide, ready, left):
    requests, steps, columns = out_ref.shape
    owners, body, width = back_ref.shape
    rows = body // QCAP
    blocks = columns // width
    few = requests // parts
    total = few * steps
    leaving = []
    for part in range(parts):
        for request in range(part * few, (part + 1) * few):
            owner, turn = seat[request] // QCAP, seat[request] % QCAP
            wide[request * rows : (request + 1) * rows, :] = back_ref[
                owner, pl.ds(pl.multiple_of(turn * rows, rows), rows), :
            ].astype(jnp.float32)
        mine = pl.ds(part * few, few)
        for c in range(blocks):
            here = slice(c * width, (c + 1) * width)
            mixed = base_ref[part * total : (part + 1) * total, here]
            mixed = mixed + wide[pl.ds(part * few * rows + c, total, stride=blocks), :]
            ready[mine, :, here] = mixed.reshape(few, steps, width).astype(ready.dtype)
        leaving.append(pltpu.make_async_copy(ready.at[mine], out_ref.at[mine], left.at[part]))
        leaving[-1].start()
    for copy in leaving:
        copy.wait()


def finish(seat, back, base, requests, steps):
    owners, body, width = back.shape
    total, columns = base.shape
    parts = FINISH if requests % FINISH == 0 else 1
    return pl.pallas_call(
        functools.partial(finish_kernel, parts),
        in_specs=[
            pl.BlockSpec(memory_space=pltpu.SMEM),
            pl.BlockSpec(memory_space=pltpu.VMEM),
            pl.BlockSpec(memory_space=pltpu.VMEM),
        ],
        out_specs=pl.BlockSpec(memory_space=pl.ANY),
        scratch_shapes=[
            pltpu.VMEM((requests * body // QCAP, width), jnp.float32),
            pltpu.VMEM((requests, steps, columns), jnp.bfloat16),
            pltpu.SemaphoreType.DMA((parts,)),
        ],
        out_shape=jax.ShapeDtypeStruct((requests, steps, columns), jnp.bfloat16),
        compiler_params=pltpu.CompilerParams(vmem_limit_bytes=SMALL_VMEM),
        cost_estimate=pl.CostEstimate(
            flops=2 * total * columns, bytes_accessed=8 * total * columns, transcendentals=0
        ),
        name="finish",
    )(seat, back, base)


def local(queries, kv_cache, new_kv, lengths, adapter_ids, place, ranks, w_out, a_store, b_store):
    request_count, step_count = (queries.shape[0], queries.shape[1])
    owners = lax.axis_size("store")
    cores = lax.axis_size("tensor")
    core = lax.axis_index("tensor")
    per_owner, feature_half, rank_width = a_store.shape
    out_half = b_store.shape[2]
    seats = owners * QCAP
    shifts = [[(k, (k + step) % cores) for k in range(cores)] for step in range(1, cores)]

    attended, sent, seat = attend(
        queries, kv_cache, new_kv, lengths, adapter_ids, place, owners, per_owner
    )
    got = lax.all_to_all(sent, "store", split_axis=0, concat_axis=0, tiled=True)

    blocks = [((core + step) % cores).reshape(1) for step in range(cores)]
    a_turned = jnp.swapaxes(a_store, 1, 2)
    here = (lax.axis_index("store") * per_owner).reshape(1)
    share, x, a_near, factor = other_columns(
        attended, w_out, blocks[1], out_half, here, place, ranks, a_turned
    )
    share = lax.ppermute(share, "tensor", shifts[0])

    own, slot = low(got, a_near, seats, step_count)
    others = jnp.stack([lax.ppermute(own, "tensor", shift) for shift in shifts])
    back = update(own, others, slot, factor, b_store, owners)
    back, x, share = lax.optimization_barrier((back, x, share))
    back = lax.all_to_all(back, "store", split_axis=0, concat_axis=0, tiled=True)
    for step in range(2, cores):
        more = own_columns(x, w_out, blocks[step], out_half, jnp.zeros_like(share))
        share = share + lax.ppermute(more, "tensor", shifts[step - 1])
    base = own_columns(x, w_out, blocks[0], out_half, share)
    return finish(seat, back, base, request_count, step_count)


def solution(mesh):
    return jax.shard_map(
        local,
        mesh=mesh,
        in_specs=(
            P(("rep", "store"), None, "tensor", None),
            P(None, ("rep", "store"), "tensor", None, None),
            P(None, ("rep", "store"), None, "tensor", None),
            P(("rep", "store")),
            P(("rep", "store")),
            P("rep"),
            P("rep"),
            P("tensor", None),
            P(("rep", "store"), "tensor", None),
            P(("rep", "store"), None, "tensor"),
        ),
        out_specs=P(("rep", "store"), None, "tensor"),
        check_vma=False,
    )
```

```python
import functools
import math

import jax
import jax.numpy as jnp
from jax import lax
from jax.experimental import pallas as pl
from jax.experimental.pallas import tpu as pltpu
from jax.sharding import PartitionSpec as P

QCAP = 3
LANES = 128
NOTE = 16
ATTEND_VMEM = 24 * 1024 * 1024
TILE = 1024
BASE_VMEM = 32 * 1024 * 1024
FINISH = 2
SMALL_VMEM = 16 * 1024 * 1024

adapter_scale = 8.0


def dot(left, right, contract=(1, 0)):
    return lax.dot_general(
        left, right, (((contract[0],), (contract[1],)), ((), ())), preferred_element_type=jnp.float32
    )


def far(x):
    return pltpu.with_memory_space_constraint(x, pltpu.HBM)


def near(x):
    return pltpu.with_memory_space_constraint(x, pltpu.VMEM)


def attend_kernel(
    sizes, heads, per_owner,
    lengths, adapter_ids, place,
    q_far, kv_far, new_far,
    attended_ref, sent_ref, seat_ref,
    q_ref, kv_ref, new_ref, taken, slots, arrived,
):
    owners = taken.shape[0]
    requests, rows, width = attended_ref.shape
    slots_in_cache = kv_ref.shape[3]
    group = heads // 2
    coming = [
        pltpu.make_async_copy(q_far, q_ref, arrived.at[0]),
        pltpu.make_async_copy(new_far, new_ref.at[:, pl.ds(0, requests)], arrived.at[1]),
    ]
    end = 0
    for size in sizes:
        few = pl.ds(end, size)
        end = end + size
        coming.append(
            pltpu.make_async_copy(kv_far.at[:, few], kv_ref.at[:, few], arrived.at[len(coming)])
        )
    for copy in coming:
        copy.start()

    for owner in range(owners):
        taken[owner] = 0
    for seat in range(owners * QCAP):
        slots[seat] = 0
    if owners * QCAP > requests:
        sent_ref[...] = jnp.zeros_like(sent_ref)

    row = lax.broadcasted_iota(jnp.int32, (rows, width), 0)
    first = (row // group) % 2 == 0
    new_count = new_ref.shape[2]
    new_row = lax.broadcasted_iota(jnp.int32, (rows, new_count), 0)
    new_column = lax.broadcasted_iota(jnp.int32, (rows, new_count), 1)
    new_seen = (new_column // 2 <= new_row // heads) & (new_column % 2 == (new_row // group) % 2)
    column = lax.broadcasted_iota(jnp.int32, (rows, slots_in_cache), 1)
    scale = 1.0 / math.sqrt(width)

    coming[0].wait()
    coming[1].wait()
    end = 0
    for size, copy in zip(sizes, coming[2:]):
        start, end = end, end + size
        copy.wait()
        cached, fresh = [], []
        for r in range(start, end):
            q = q_ref[r]
            q_wide = q.astype(jnp.float32)
            both = jnp.concatenate(
                [jnp.where(first, q_wide, 0.0), jnp.where(first, 0.0, q_wide)], axis=1
            ).astype(jnp.bfloat16)
            keys = jnp.concatenate([kv_ref[0, r, 0], kv_ref[0, r, 1]], axis=1)
            scores = dot(both, keys, (1, 1)) * scale
            cached.append(jnp.where(column < lengths[r], scores, -jnp.inf))
            scores = dot(q, new_ref[0, r], (1, 1)) * scale
            fresh.append(jnp.where(new_seen, scores, -jnp.inf))
        tops = [
            jnp.maximum(jnp.max(a, axis=1, keepdims=True), jnp.max(b, axis=1, keepdims=True))
            for a, b in zip(cached, fresh)
        ]
        cached = [jnp.exp(a - top) for a, top in zip(cached, tops)]
        fresh = [jnp.exp(b - top) for b, top in zip(fresh, tops)]
        sums = [
            1.0 / (jnp.sum(a, axis=1, keepdims=True) + jnp.sum(b, axis=1, keepdims=True))
            for a, b in zip(cached, fresh)
        ]
        cached = [(a * inv).astype(jnp.bfloat16) for a, inv in zip(cached, sums)]
        fresh = [(b * inv).astype(jnp.bfloat16) for b, inv in zip(fresh, sums)]
        for a, b, r in zip(cached, fresh, range(start, end)):
            values = jnp.concatenate([kv_ref[1, r, 0], kv_ref[1, r, 1]], axis=1)
            both = dot(a, values)
            result = jnp.where(first, both[:, :width], both[:, width:]) + dot(b, new_ref[1, r])
            result = result.astype(jnp.bfloat16)
            location = place[adapter_ids[r]]
            owner = location // per_owner
            turn = taken[owner]
            taken[owner] = turn + 1
            slots[owner * QCAP + turn] = location % per_owner
            seat_ref[r] = owner * QCAP + turn
            attended_ref[r] = result
            sent_ref[owner, pl.ds(pl.multiple_of(turn * rows, rows), rows), :] = result

    note_row = lax.broadcasted_iota(jnp.int32, (NOTE, width), 0)
    per_seat = rows // heads
    for owner in range(owners):
        note = jnp.zeros((NOTE, width), jnp.int32)
        for turn in range(QCAP):
            note = jnp.where(note_row // per_seat == turn, slots[owner * QCAP + turn], note)
        sent_ref[owner, QCAP * rows :, :] = note.astype(jnp.float32).astype(jnp.bfloat16)


def attend(queries, kv_cache, new_kv, lengths, adapter_ids, place, owners, per_owner):
    requests, step_count, heads, width = queries.shape
    rows = step_count * heads
    new_rows = new_kv.shape[2] * new_kv.shape[3]
    body = QCAP * rows + NOTE
    sizes = [requests // 6, requests // 3]
    sizes = [size for size in [*sizes, requests - sum(sizes)] if size]
    queries = queries.reshape(requests, rows, width)
    new_kv = new_kv.reshape(2, requests, new_rows, width)
    anywhere = pl.BlockSpec(memory_space=pl.ANY)
    return pl.pallas_call(
        functools.partial(attend_kernel, sizes, heads, per_owner),
        grid_spec=pltpu.PrefetchScalarGridSpec(
            num_scalar_prefetch=3,
            grid=(1,),
            in_specs=[anywhere, anywhere, anywhere],
            out_specs=[
                pl.BlockSpec(memory_space=pltpu.VMEM),
                pl.BlockSpec((owners, body, width), lambda i, *_: (0, 0, 0)),
                pl.BlockSpec(memory_space=pltpu.SMEM),
            ],
            scratch_shapes=[
                pltpu.VMEM(queries.shape, queries.dtype),
                pltpu.VMEM(kv_cache.shape, kv_cache.dtype),
                pltpu.VMEM((2, requests + 1, new_rows, width), new_kv.dtype),
                pltpu.SMEM((owners,), jnp.int32),
                pltpu.SMEM((owners * QCAP,), jnp.int32),
                pltpu.SemaphoreType.DMA((2 + len(sizes),)),
            ],
        ),
        out_shape=[
            pltpu.VMEM((requests, rows, width), jnp.bfloat16),
            pltpu.HBM((owners, body, width), jnp.bfloat16),
            jax.ShapeDtypeStruct((requests,), jnp.int32),
        ],
        compiler_params=pltpu.CompilerParams(
            dimension_semantics=("arbitrary",), vmem_limit_bytes=ATTEND_VMEM
        ),
        cost_estimate=pl.CostEstimate(
            flops=4 * requests * rows * kv_cache.shape[3] * width * 2,
            bytes_accessed=kv_cache.size * 2 + 4 * queries.size,
            transcendentals=requests * rows * kv_cache.shape[3],
        ),
        name="attend",
    )(far(lengths), far(adapter_ids), far(place), far(queries), far(kv_cache), far(new_kv))


def other_columns_kernel(
    block, here, place, ranks,
    attended_ref, w_ref, a_ref,
    out_ref, x_ref, a_near, factor_ref,
    wide, arrived,
):
    copy = pltpu.make_async_copy(a_ref, a_near, arrived)
    last = pl.program_id(0) == pl.num_programs(0) - 1

    @pl.when(pl.program_id(0) == 0)
    def _():
        total, width = x_ref.shape[0], wide.shape[1]
        blocks = x_ref.shape[1] // width
        wide[...] = attended_ref[...].reshape(wide.shape).astype(jnp.float32)
        for c in range(blocks):
            x_ref[:, c * width : (c + 1) * width] = wide[pl.ds(c, total, stride=blocks), :].astype(
                jnp.bfloat16
            )

    @pl.when(last)
    def _():
        copy.start()

    out_ref[...] = dot(x_ref[...], w_ref[...])

    @pl.when(last)
    def _():
        rank_width = a_ref.shape[1]
        part = lax.broadcasted_iota(jnp.int32, factor_ref.shape, 0)
        lane = lax.broadcasted_iota(jnp.int32, factor_ref.shape, 1)
        position = here[0] + (part * factor_ref.shape[1] + lane) // rank_width
        rank = jnp.zeros(factor_ref.shape, jnp.int32)
        for adapter in range(place.shape[0]):
            rank = rank + jnp.where(position == place[adapter], ranks[adapter], 0)
        scale = adapter_scale / jnp.sqrt(rank.astype(jnp.float32))
        factor_ref[...] = jnp.where(lane % rank_width < rank, scale, 0.0)
        copy.wait()


def other_columns(attended, w_out, block, columns, here, place, ranks, a_turned):
    requests, rows, width = attended.shape
    features = w_out.shape[0]
    total = requests * rows * width // features
    tile = min(TILE, columns)
    steps = columns // tile
    parts = a_turned.shape[0] * a_turned.shape[1] // width
    whole = pl.BlockSpec(memory_space=pltpu.VMEM)
    return pl.pallas_call(
        other_columns_kernel,
        grid_spec=pltpu.PrefetchScalarGridSpec(
            num_scalar_prefetch=4,
            grid=(steps,),
            in_specs=[
                whole,
                pl.BlockSpec((features, tile), lambda i, block, *_: (0, block[0] * steps + i)),
                pl.BlockSpec(memory_space=pl.ANY),
            ],
            out_specs=[
                pl.BlockSpec((total, tile), lambda i, *_: (0, i)),
                pl.BlockSpec((total, features), lambda i, *_: (0, 0)),
                whole,
                whole,
            ],
            scratch_shapes=[
                pltpu.VMEM((requests * rows, width), jnp.float32),
                pltpu.SemaphoreType.DMA,
            ],
        ),
        out_shape=[
            jax.ShapeDtypeStruct((total, columns), jnp.float32),
            pltpu.HBM((total, features), jnp.bfloat16),
            pltpu.VMEM(a_turned.shape, a_turned.dtype),
            pltpu.VMEM((parts, width), jnp.float32),
        ],
        compiler_params=pltpu.CompilerParams(
            dimension_semantics=("arbitrary",), vmem_limit_bytes=BASE_VMEM
        ),
        cost_estimate=pl.CostEstimate(
            flops=2 * total * features * columns,
            bytes_accessed=2 * features * columns + 4 * a_turned.size,
            transcendentals=0,
        ),
        name="other_columns",
    )(block, here, far(place), far(ranks), near(attended), far(w_out), far(a_turned))


def own_columns_kernel(block, x_ref, w_ref, share_ref, out_ref):
    out_ref[...] = dot(x_ref[...], w_ref[...]) + share_ref[...]


def own_columns(x, w_out, block, columns, share):
    total, features = x.shape
    tile = min(TILE, columns)
    steps = columns // tile
    return pl.pallas_call(
        own_columns_kernel,
        grid_spec=pltpu.PrefetchScalarGridSpec(
            num_scalar_prefetch=1,
            grid=(steps,),
            in_specs=[
                pl.BlockSpec((total, features), lambda i, block: (0, 0)),
                pl.BlockSpec((features, tile), lambda i, block: (0, block[0] * steps + i)),
                pl.BlockSpec((total, tile), lambda i, block: (0, i)),
            ],
            out_specs=pl.BlockSpec((total, tile), lambda i, block: (0, i)),
        ),
        out_shape=jax.ShapeDtypeStruct((total, columns), jnp.float32),
        compiler_params=pltpu.CompilerParams(
            dimension_semantics=("arbitrary",), vmem_limit_bytes=BASE_VMEM
        ),
        cost_estimate=pl.CostEstimate(
            flops=2 * total * features * columns, bytes_accessed=2 * features * columns, transcendentals=0
        ),
        name="own_columns",
    )(block, far(x), far(w_out), share)


def low_kernel(seats, steps, got_ref, a_ref, low_ref, slot_ref, wide, spare):
    owners, rows, width = got_ref.shape
    body = rows - NOTE
    per_owner, rank_width, features = a_ref.shape
    for owner in range(owners):
        wide[owner * body : (owner + 1) * body, :] = got_ref[owner, :body, :].astype(jnp.float32)
    blocks = features // width
    total = seats * steps
    x = jnp.concatenate(
        [wide[pl.ds(c, total, stride=blocks), :].astype(jnp.bfloat16) for c in range(blocks)], axis=1
    )
    per_group = total // owners
    for owner in range(owners):
        spare[owner * per_group : (owner + 1) * per_group, :] = got_ref[owner, body:, :].astype(
            jnp.float32
        )[:per_group]
    every = dot(x, a_ref[...].reshape(per_owner * rank_width, features), (1, 1))
    slot_ref[...] = spare[:total]
    slot = spare[:total].astype(jnp.int32)
    lane = lax.broadcasted_iota(jnp.int32, (total, width), 1)
    per_block = width // rank_width
    kept = jnp.zeros((total, width), jnp.float32)
    for c in range(per_owner // per_block):
        mine = slot == c * per_block + lane // rank_width
        kept = kept + jnp.where(mine, every[:, c * width : (c + 1) * width], 0.0)
    folded = kept
    for k in range(1, per_block):
        folded = folded + pltpu.roll(kept, k * rank_width, 1)
    low_ref[...] = folded


def low(got, a_turned, seats, steps):
    owners, rows, width = got.shape
    total = seats * steps
    return pl.pallas_call(
        functools.partial(low_kernel, seats, steps),
        out_shape=[
            jax.ShapeDtypeStruct((total, width), jnp.float32),
            jax.ShapeDtypeStruct((total, width), jnp.float32),
        ],
        in_specs=[pl.BlockSpec(memory_space=pltpu.VMEM)] * 2,
        out_specs=[pl.BlockSpec(memory_space=pltpu.VMEM)] * 2,
        scratch_shapes=[
            pltpu.VMEM((owners * (rows - NOTE), width), jnp.float32),
            pltpu.VMEM((total + NOTE, width), jnp.float32),
        ],
        compiler_params=pltpu.CompilerParams(vmem_limit_bytes=SMALL_VMEM),
        cost_estimate=pl.CostEstimate(
            flops=2 * total * a_turned.size, bytes_accessed=2 * a_turned.size, transcendentals=0
        ),
        name="low",
    )(got, near(a_turned))


def update_kernel(own_ref, other_ref, slot_ref, factor_ref, b_ref, back_ref, wide, ready, left):
    total, width = own_ref.shape
    per_owner, rank_width, columns = b_ref.shape
    owners, body, _ = back_ref.shape
    per_block = width // rank_width
    blocks = columns // width
    parts = per_owner // per_block
    summed = own_ref[...]
    for k in range(other_ref.shape[0]):
        summed = summed + other_ref[k]
    slot = slot_ref[...].astype(jnp.int32)
    lane = lax.broadcasted_iota(jnp.int32, (total, width), 1)
    spread = []
    for c in range(parts):
        mine = slot == c * per_block + lane // rank_width
        scaled = summed * factor_ref[c : c + 1, :]
        spread.append(jnp.where(mine, scaled, 0.0).astype(jnp.bfloat16))
    spread = jnp.concatenate(spread, axis=1)
    result = dot(spread, b_ref[...].reshape(per_owner * rank_width, columns))
    for c in range(blocks):
        wide[pl.ds(c, total, stride=blocks), :] = result[:, c * width : (c + 1) * width]
    half = owners // 2
    leaving = []
    for start, end in ((0, half), (half, owners)):
        for owner in range(start, end):
            ready[owner] = wide[owner * body : (owner + 1) * body, :].astype(jnp.bfloat16)
        few = pl.ds(start, end - start)
        leaving.append(pltpu.make_async_copy(ready.at[few], back_ref.at[few], left.at[len(leaving)]))
        leaving[-1].start()
    for copy in leaving:
        copy.wait()


def update(own, others, slot, factor, b_store, owners):
    total, width = own.shape
    columns = b_store.shape[2]
    body = total * columns // width // owners
    return pl.pallas_call(
        update_kernel,
        out_shape=pltpu.HBM((owners, body, width), jnp.bfloat16),
        in_specs=[pl.BlockSpec(memory_space=pltpu.VMEM)] * 5,
        out_specs=pl.BlockSpec(memory_space=pl.ANY),
        scratch_shapes=[
            pltpu.VMEM((owners * body, width), jnp.float32),
            pltpu.VMEM((owners, body, width), jnp.bfloat16),
            pltpu.SemaphoreType.DMA((2,)),
        ],
        compiler_params=pltpu.CompilerParams(vmem_limit_bytes=SMALL_VMEM),
        cost_estimate=pl.CostEstimate(
            flops=2 * total * b_store.size, bytes_accessed=2 * b_store.size, transcendentals=0
        ),
        name="update",
    )(own, others, slot, near(factor), near(b_store))


def finish_kernel(parts, seat, back_ref, base_ref, out_ref, wide, ready, left):
    requests, steps, columns = out_ref.shape
    owners, body, width = back_ref.shape
    rows = body // QCAP
    blocks = columns // width
    few = requests // parts
    total = few * steps
    leaving = []
    for part in range(parts):
        for request in range(part * few, (part + 1) * few):
            owner, turn = seat[request] // QCAP, seat[request] % QCAP
            wide[request * rows : (request + 1) * rows, :] = back_ref[
                owner, pl.ds(pl.multiple_of(turn * rows, rows), rows), :
            ].astype(jnp.float32)
        mine = pl.ds(part * few, few)
        for c in range(blocks):
            here = slice(c * width, (c + 1) * width)
            mixed = base_ref[part * total : (part + 1) * total, here]
            mixed = mixed + wide[pl.ds(part * few * rows + c, total, stride=blocks), :]
            ready[mine, :, here] = mixed.reshape(few, steps, width).astype(ready.dtype)
        leaving.append(pltpu.make_async_copy(ready.at[mine], out_ref.at[mine], left.at[part]))
        leaving[-1].start()
    for copy in leaving:
        copy.wait()


def finish(seat, back, base, requests, steps):
    owners, body, width = back.shape
    total, columns = base.shape
    parts = FINISH if requests % FINISH == 0 else 1
    return pl.pallas_call(
        functools.partial(finish_kernel, parts),
        in_specs=[
            pl.BlockSpec(memory_space=pltpu.SMEM),
            pl.BlockSpec(memory_space=pltpu.VMEM),
            pl.BlockSpec(memory_space=pltpu.VMEM),
        ],
        out_specs=pl.BlockSpec(memory_space=pl.ANY),
        scratch_shapes=[
            pltpu.VMEM((requests * body // QCAP, width), jnp.float32),
            pltpu.VMEM((requests + 2, steps, columns), jnp.bfloat16),
            pltpu.SemaphoreType.DMA((parts,)),
        ],
        out_shape=jax.ShapeDtypeStruct((requests, steps, columns), jnp.bfloat16),
        compiler_params=pltpu.CompilerParams(vmem_limit_bytes=SMALL_VMEM),
        cost_estimate=pl.CostEstimate(
            flops=2 * total * columns, bytes_accessed=8 * total * columns, transcendentals=0
        ),
        name="finish",
    )(seat, back, base)


def local(queries, kv_cache, new_kv, lengths, adapter_ids, place, ranks, w_out, a_store, b_store):
    request_count, step_count = (queries.shape[0], queries.shape[1])
    owners = lax.axis_size("store")
    cores = lax.axis_size("tensor")
    core = lax.axis_index("tensor")
    per_owner, feature_half, rank_width = a_store.shape
    out_half = b_store.shape[2]
    seats = owners * QCAP
    shifts = [[(k, (k + step) % cores) for k in range(cores)] for step in range(1, cores)]

    attended, sent, seat = attend(
        queries, kv_cache, new_kv, lengths, adapter_ids, place, owners, per_owner
    )
    got = lax.all_to_all(sent, "store", split_axis=0, concat_axis=0, tiled=True)

    blocks = [((core + step) % cores).reshape(1) for step in range(cores)]
    a_turned = jnp.swapaxes(a_store, 1, 2)
    here = (lax.axis_index("store") * per_owner).reshape(1)
    share, x, a_near, factor = other_columns(
        attended, w_out, blocks[1], out_half, here, place, ranks, a_turned
    )
    share = lax.ppermute(share, "tensor", shifts[0])

    own, slot = low(got, a_near, seats, step_count)
    others = jnp.stack([lax.ppermute(own, "tensor", shift) for shift in shifts])
    back = update(own, others, slot, factor, b_store, owners)
    back, x, share = lax.optimization_barrier((back, x, share))
    back = lax.all_to_all(back, "store", split_axis=0, concat_axis=0, tiled=True)
    for step in range(2, cores):
        more = own_columns(x, w_out, blocks[step], out_half, jnp.zeros_like(share))
        share = share + lax.ppermute(more, "tensor", shifts[step - 1])
    base = own_columns(x, w_out, blocks[0], out_half, share)
    return finish(seat, back, base, request_count, step_count)


def solution(mesh):
    return jax.shard_map(
        local,
        mesh=mesh,
        in_specs=(
            P(("rep", "store"), None, "tensor", None),
            P(None, ("rep", "store"), "tensor", None, None),
            P(None, ("rep", "store"), None, "tensor", None),
            P(("rep", "store")),
            P(("rep", "store")),
            P("rep"),
            P("rep"),
            P("tensor", None),
            P(("rep", "store"), "tensor", None),
            P(("rep", "store"), None, "tensor"),
        ),
        out_specs=P(("rep", "store"), None, "tensor"),
        check_vma=False,
    )
```

```python
import functools
import math

import jax
import jax.numpy as jnp
from jax import lax
from jax.experimental import pallas as pl
from jax.experimental.pallas import tpu as pltpu
from jax.sharding import PartitionSpec as P

QCAP = 3
LANES = 128
NOTE = 16
ATTEND_VMEM = 24 * 1024 * 1024
TILE = 1024
BASE_VMEM = 32 * 1024 * 1024
FINISH = 2
SMALL_VMEM = 16 * 1024 * 1024

adapter_scale = 8.0


def dot(left, right, contract=(1, 0)):
    return lax.dot_general(
        left, right, (((contract[0],), (contract[1],)), ((), ())), preferred_element_type=jnp.float32
    )


def far(x):
    return pltpu.with_memory_space_constraint(x, pltpu.HBM)


def near(x):
    return pltpu.with_memory_space_constraint(x, pltpu.VMEM)


def attend_kernel(
    sizes, heads, per_owner,
    lengths, adapter_ids, place,
    q_far, kv_far, new_far,
    attended_ref, sent_ref, seat_ref,
    q_ref, kv_ref, new_ref, taken, slots, arrived,
):
    owners = taken.shape[0]
    requests, rows, width = attended_ref.shape
    slots_in_cache = kv_ref.shape[3]
    group = heads // 2
    coming = [
        pltpu.make_async_copy(q_far, q_ref, arrived.at[0]),
        pltpu.make_async_copy(new_far, new_ref.at[:, pl.ds(0, requests)], arrived.at[1]),
    ]
    end = 0
    for size in sizes:
        few = pl.ds(end, size)
        end = end + size
        coming.append(
            pltpu.make_async_copy(kv_far.at[:, few], kv_ref.at[:, few], arrived.at[len(coming)])
        )
    for copy in coming:
        copy.start()

    for owner in range(owners):
        taken[owner] = 0
    for seat in range(owners * QCAP):
        slots[seat] = 0
    if owners * QCAP > requests:
        sent_ref[...] = jnp.zeros_like(sent_ref)

    row = lax.broadcasted_iota(jnp.int32, (rows, width), 0)
    first = (row // group) % 2 == 0
    new_count = new_ref.shape[2]
    new_row = lax.broadcasted_iota(jnp.int32, (rows, new_count), 0)
    new_column = lax.broadcasted_iota(jnp.int32, (rows, new_count), 1)
    new_seen = (new_column // 2 <= new_row // heads) & (new_column % 2 == (new_row // group) % 2)
    column = lax.broadcasted_iota(jnp.int32, (rows, slots_in_cache), 1)
    scale = 1.0 / math.sqrt(width)

    coming[0].wait()
    coming[1].wait()
    end = 0
    for size, copy in zip(sizes, coming[2:]):
        start, end = end, end + size
        copy.wait()
        cached, fresh = [], []
        for r in range(start, end):
            q = q_ref[r]
            q_wide = q.astype(jnp.float32)
            both = jnp.concatenate(
                [jnp.where(first, q_wide, 0.0), jnp.where(first, 0.0, q_wide)], axis=1
            ).astype(jnp.bfloat16)
            keys = jnp.concatenate([kv_ref[0, r, 0], kv_ref[0, r, 1]], axis=1)
            scores = dot(both, keys, (1, 1)) * scale
            cached.append(jnp.where(column < lengths[r], scores, -jnp.inf))
            scores = dot(q, new_ref[0, r], (1, 1)) * scale
            fresh.append(jnp.where(new_seen, scores, -jnp.inf))
        tops = [
            jnp.maximum(jnp.max(a, axis=1, keepdims=True), jnp.max(b, axis=1, keepdims=True))
            for a, b in zip(cached, fresh)
        ]
        cached = [jnp.exp(a - top) for a, top in zip(cached, tops)]
        fresh = [jnp.exp(b - top) for b, top in zip(fresh, tops)]
        sums = [
            1.0 / (jnp.sum(a, axis=1, keepdims=True) + jnp.sum(b, axis=1, keepdims=True))
            for a, b in zip(cached, fresh)
        ]
        cached = [a.astype(jnp.bfloat16) for a in cached]
        fresh = [b.astype(jnp.bfloat16) for b in fresh]
        for a, b, inv, r in zip(cached, fresh, sums, range(start, end)):
            values = jnp.concatenate([kv_ref[1, r, 0], kv_ref[1, r, 1]], axis=1)
            both = dot(a, values)
            result = jnp.where(first, both[:, :width], both[:, width:]) + dot(b, new_ref[1, r])
            result = (result * inv).astype(jnp.bfloat16)
            location = place[adapter_ids[r]]
            owner = location // per_owner
            turn = taken[owner]
            taken[owner] = turn + 1
            slots[owner * QCAP + turn] = location % per_owner
            seat_ref[r] = owner * QCAP + turn
            attended_ref[r] = result
            sent_ref[owner, pl.ds(pl.multiple_of(turn * rows, rows), rows), :] = result

    note_row = lax.broadcasted_iota(jnp.int32, (NOTE, width), 0)
    per_seat = rows // heads
    for owner in range(owners):
        note = jnp.zeros((NOTE, width), jnp.int32)
        for turn in range(QCAP):
            note = jnp.where(note_row // per_seat == turn, slots[owner * QCAP + turn], note)
        sent_ref[owner, QCAP * rows :, :] = note.astype(jnp.float32).astype(jnp.bfloat16)


def attend(queries, kv_cache, new_kv, lengths, adapter_ids, place, owners, per_owner):
    requests, step_count, heads, width = queries.shape
    rows = step_count * heads
    new_rows = new_kv.shape[2] * new_kv.shape[3]
    body = QCAP * rows + NOTE
    sizes = [requests // 6, requests // 3]
    sizes = [size for size in [*sizes, requests - sum(sizes)] if size]
    queries = queries.reshape(requests, rows, width)
    new_kv = new_kv.reshape(2, requests, new_rows, width)
    anywhere = pl.BlockSpec(memory_space=pl.ANY)
    return pl.pallas_call(
        functools.partial(attend_kernel, sizes, heads, per_owner),
        grid_spec=pltpu.PrefetchScalarGridSpec(
            num_scalar_prefetch=3,
            grid=(1,),
            in_specs=[anywhere, anywhere, anywhere],
            out_specs=[
                pl.BlockSpec(memory_space=pltpu.VMEM),
                pl.BlockSpec((owners, body, width), lambda i, *_: (0, 0, 0)),
                pl.BlockSpec(memory_space=pltpu.SMEM),
            ],
            scratch_shapes=[
                pltpu.VMEM(queries.shape, queries.dtype),
                pltpu.VMEM(kv_cache.shape, kv_cache.dtype),
                pltpu.VMEM((2, requests + 1, new_rows, width), new_kv.dtype),
                pltpu.SMEM((owners,), jnp.int32),
                pltpu.SMEM((owners * QCAP,), jnp.int32),
                pltpu.SemaphoreType.DMA((2 + len(sizes),)),
            ],
        ),
        out_shape=[
            pltpu.VMEM((requests, rows, width), jnp.bfloat16),
            pltpu.HBM((owners, body, width), jnp.bfloat16),
            jax.ShapeDtypeStruct((requests,), jnp.int32),
        ],
        compiler_params=pltpu.CompilerParams(
            dimension_semantics=("arbitrary",), vmem_limit_bytes=ATTEND_VMEM
        ),
        cost_estimate=pl.CostEstimate(
            flops=4 * requests * rows * kv_cache.shape[3] * width * 2,
            bytes_accessed=kv_cache.size * 2 + 4 * queries.size,
            transcendentals=requests * rows * kv_cache.shape[3],
        ),
        name="attend",
    )(far(lengths), far(adapter_ids), far(place), far(queries), far(kv_cache), far(new_kv))


def other_columns_kernel(
    block, here, place, ranks,
    attended_ref, w_ref, a_ref,
    out_ref, x_ref, a_near, factor_ref,
    wide, arrived,
):
    copy = pltpu.make_async_copy(a_ref, a_near, arrived)
    last = pl.program_id(0) == pl.num_programs(0) - 1

    @pl.when(pl.program_id(0) == 0)
    def _():
        total, width = x_ref.shape[0], wide.shape[1]
        blocks = x_ref.shape[1] // width
        wide[...] = attended_ref[...].reshape(wide.shape).astype(jnp.float32)
        for c in range(blocks):
            x_ref[:, c * width : (c + 1) * width] = wide[pl.ds(c, total, stride=blocks), :].astype(
                jnp.bfloat16
            )

    @pl.when(last)
    def _():
        copy.start()

    out_ref[...] = dot(x_ref[...], w_ref[...])

    @pl.when(last)
    def _():
        rank_width = a_ref.shape[1]
        part = lax.broadcasted_iota(jnp.int32, factor_ref.shape, 0)
        lane = lax.broadcasted_iota(jnp.int32, factor_ref.shape, 1)
        position = here[0] + (part * factor_ref.shape[1] + lane) // rank_width
        rank = jnp.zeros(factor_ref.shape, jnp.int32)
        for adapter in range(place.shape[0]):
            rank = rank + jnp.where(position == place[adapter], ranks[adapter], 0)
        scale = adapter_scale / jnp.sqrt(rank.astype(jnp.float32))
        factor_ref[...] = jnp.where(lane % rank_width < rank, scale, 0.0)
        copy.wait()


def other_columns(attended, w_out, block, columns, here, place, ranks, a_turned):
    requests, rows, width = attended.shape
    features = w_out.shape[0]
    total = requests * rows * width // features
    tile = min(TILE, columns)
    steps = columns // tile
    parts = a_turned.shape[0] * a_turned.shape[1] // width
    whole = pl.BlockSpec(memory_space=pltpu.VMEM)
    return pl.pallas_call(
        other_columns_kernel,
        grid_spec=pltpu.PrefetchScalarGridSpec(
            num_scalar_prefetch=4,
            grid=(steps,),
            in_specs=[
                whole,
                pl.BlockSpec((features, tile), lambda i, block, *_: (0, block[0] * steps + i)),
                pl.BlockSpec(memory_space=pl.ANY),
            ],
            out_specs=[
                pl.BlockSpec((total, tile), lambda i, *_: (0, i)),
                pl.BlockSpec((total, features), lambda i, *_: (0, 0)),
                whole,
                whole,
            ],
            scratch_shapes=[
                pltpu.VMEM((requests * rows, width), jnp.float32),
                pltpu.SemaphoreType.DMA,
            ],
        ),
        out_shape=[
            jax.ShapeDtypeStruct((total, columns), jnp.float32),
            pltpu.HBM((total, features), jnp.bfloat16),
            pltpu.VMEM(a_turned.shape, a_turned.dtype),
            pltpu.VMEM((parts, width), jnp.float32),
        ],
        compiler_params=pltpu.CompilerParams(
            dimension_semantics=("arbitrary",), vmem_limit_bytes=BASE_VMEM
        ),
        cost_estimate=pl.CostEstimate(
            flops=2 * total * features * columns,
            bytes_accessed=2 * features * columns + 4 * a_turned.size,
            transcendentals=0,
        ),
        name="other_columns",
    )(block, here, far(place), far(ranks), near(attended), far(w_out), far(a_turned))


def own_columns_kernel(block, x_ref, w_ref, share_ref, out_ref):
    out_ref[...] = dot(x_ref[...], w_ref[...]) + share_ref[...]


def own_columns(x, w_out, block, columns, share):
    total, features = x.shape
    tile = min(TILE, columns)
    steps = columns // tile
    return pl.pallas_call(
        own_columns_kernel,
        grid_spec=pltpu.PrefetchScalarGridSpec(
            num_scalar_prefetch=1,
            grid=(steps,),
            in_specs=[
                pl.BlockSpec((total, features), lambda i, block: (0, 0)),
                pl.BlockSpec((features, tile), lambda i, block: (0, block[0] * steps + i)),
                pl.BlockSpec((total, tile), lambda i, block: (0, i)),
            ],
            out_specs=pl.BlockSpec((total, tile), lambda i, block: (0, i)),
        ),
        out_shape=jax.ShapeDtypeStruct((total, columns), jnp.float32),
        compiler_params=pltpu.CompilerParams(
            dimension_semantics=("arbitrary",), vmem_limit_bytes=BASE_VMEM
        ),
        cost_estimate=pl.CostEstimate(
            flops=2 * total * features * columns, bytes_accessed=2 * features * columns, transcendentals=0
        ),
        name="own_columns",
    )(block, far(x), far(w_out), share)


def low_kernel(seats, steps, got_ref, a_ref, low_ref, slot_ref, wide, spare):
    owners, rows, width = got_ref.shape
    body = rows - NOTE
    per_owner, rank_width, features = a_ref.shape
    for owner in range(owners):
        wide[owner * body : (owner + 1) * body, :] = got_ref[owner, :body, :].astype(jnp.float32)
    blocks = features // width
    total = seats * steps
    x = jnp.concatenate(
        [wide[pl.ds(c, total, stride=blocks), :].astype(jnp.bfloat16) for c in range(blocks)], axis=1
    )
    per_group = total // owners
    for owner in range(owners):
        spare[owner * per_group : (owner + 1) * per_group, :] = got_ref[owner, body:, :].astype(
            jnp.float32
        )[:per_group]
    every = dot(x, a_ref[...].reshape(per_owner * rank_width, features), (1, 1))
    slot_ref[...] = spare[:total]
    slot = spare[:total].astype(jnp.int32)
    lane = lax.broadcasted_iota(jnp.int32, (total, width), 1)
    per_block = width // rank_width
    kept = jnp.zeros((total, width), jnp.float32)
    for c in range(per_owner // per_block):
        mine = slot == c * per_block + lane // rank_width
        kept = kept + jnp.where(mine, every[:, c * width : (c + 1) * width], 0.0)
    folded = kept
    for k in range(1, per_block):
        folded = folded + pltpu.roll(kept, k * rank_width, 1)
    low_ref[...] = folded


def low(got, a_turned, seats, steps):
    owners, rows, width = got.shape
    total = seats * steps
    return pl.pallas_call(
        functools.partial(low_kernel, seats, steps),
        out_shape=[
            jax.ShapeDtypeStruct((total, width), jnp.float32),
            jax.ShapeDtypeStruct((total, width), jnp.float32),
        ],
        in_specs=[pl.BlockSpec(memory_space=pltpu.VMEM)] * 2,
        out_specs=[pl.BlockSpec(memory_space=pltpu.VMEM)] * 2,
        scratch_shapes=[
            pltpu.VMEM((owners * (rows - NOTE), width), jnp.float32),
            pltpu.VMEM((total + NOTE, width), jnp.float32),
        ],
        compiler_params=pltpu.CompilerParams(vmem_limit_bytes=SMALL_VMEM),
        cost_estimate=pl.CostEstimate(
            flops=2 * total * a_turned.size, bytes_accessed=2 * a_turned.size, transcendentals=0
        ),
        name="low",
    )(got, near(a_turned))


def update_kernel(own_ref, other_ref, slot_ref, factor_ref, b_ref, back_ref, wide, ready, left):
    total, width = own_ref.shape
    per_owner, rank_width, columns = b_ref.shape
    owners, body, _ = back_ref.shape
    per_block = width // rank_width
    blocks = columns // width
    parts = per_owner // per_block
    summed = own_ref[...]
    for k in range(other_ref.shape[0]):
        summed = summed + other_ref[k]
    slot = slot_ref[...].astype(jnp.int32)
    lane = lax.broadcasted_iota(jnp.int32, (total, width), 1)
    spread = []
    for c in range(parts):
        mine = slot == c * per_block + lane // rank_width
        scaled = summed * factor_ref[c : c + 1, :]
        spread.append(jnp.where(mine, scaled, 0.0).astype(jnp.bfloat16))
    spread = jnp.concatenate(spread, axis=1)
    result = dot(spread, b_ref[...].reshape(per_owner * rank_width, columns))
    for c in range(blocks):
        wide[pl.ds(c, total, stride=blocks), :] = result[:, c * width : (c + 1) * width]
    half = owners // 2
    leaving = []
    for start, end in ((0, half), (half, owners)):
        for owner in range(start, end):
            ready[owner] = wide[owner * body : (owner + 1) * body, :].astype(jnp.bfloat16)
        few = pl.ds(start, end - start)
        leaving.append(pltpu.make_async_copy(ready.at[few], back_ref.at[few], left.at[len(leaving)]))
        leaving[-1].start()
    for copy in leaving:
        copy.wait()


def update(own, others, slot, factor, b_store, owners):
    total, width = own.shape
    columns = b_store.shape[2]
    body = total * columns // width // owners
    return pl.pallas_call(
        update_kernel,
        out_shape=pltpu.HBM((owners, body, width), jnp.bfloat16),
        in_specs=[pl.BlockSpec(memory_space=pltpu.VMEM)] * 5,
        out_specs=pl.BlockSpec(memory_space=pl.ANY),
        scratch_shapes=[
            pltpu.VMEM((owners * body, width), jnp.float32),
            pltpu.VMEM((owners, body, width), jnp.bfloat16),
            pltpu.SemaphoreType.DMA((2,)),
        ],
        compiler_params=pltpu.CompilerParams(vmem_limit_bytes=SMALL_VMEM),
        cost_estimate=pl.CostEstimate(
            flops=2 * total * b_store.size, bytes_accessed=2 * b_store.size, transcendentals=0
        ),
        name="update",
    )(own, others, slot, near(factor), near(b_store))


def finish_kernel(parts, seat, back_ref, base_ref, out_ref, wide, ready, left):
    requests, steps, columns = out_ref.shape
    owners, body, width = back_ref.shape
    rows = body // QCAP
    blocks = columns // width
    few = requests // parts
    total = few * steps
    leaving = []
    for part in range(parts):
        for request in range(part * few, (part + 1) * few):
            owner, turn = seat[request] // QCAP, seat[request] % QCAP
            wide[request * rows : (request + 1) * rows, :] = back_ref[
                owner, pl.ds(pl.multiple_of(turn * rows, rows), rows), :
            ].astype(jnp.float32)
        mine = pl.ds(part * few, few)
        for c in range(blocks):
            here = slice(c * width, (c + 1) * width)
            mixed = base_ref[part * total : (part + 1) * total, here]
            mixed = mixed + wide[pl.ds(part * few * rows + c, total, stride=blocks), :]
            ready[mine, :, here] = mixed.reshape(few, steps, width).astype(ready.dtype)
        leaving.append(pltpu.make_async_copy(ready.at[mine], out_ref.at[mine], left.at[part]))
        leaving[-1].start()
    for copy in leaving:
        copy.wait()


def finish(seat, back, base, requests, steps):
    owners, body, width = back.shape
    total, columns = base.shape
    parts = FINISH if requests % FINISH == 0 else 1
    return pl.pallas_call(
        functools.partial(finish_kernel, parts),
        in_specs=[
            pl.BlockSpec(memory_space=pltpu.SMEM),
            pl.BlockSpec(memory_space=pltpu.VMEM),
            pl.BlockSpec(memory_space=pltpu.VMEM),
        ],
        out_specs=pl.BlockSpec(memory_space=pl.ANY),
        scratch_shapes=[
            pltpu.VMEM((requests * body // QCAP, width), jnp.float32),
            pltpu.VMEM((requests + 2, steps, columns), jnp.bfloat16),
            pltpu.SemaphoreType.DMA((parts,)),
        ],
        out_shape=jax.ShapeDtypeStruct((requests, steps, columns), jnp.bfloat16),
        compiler_params=pltpu.CompilerParams(vmem_limit_bytes=SMALL_VMEM),
        cost_estimate=pl.CostEstimate(
            flops=2 * total * columns, bytes_accessed=8 * total * columns, transcendentals=0
        ),
        name="finish",
    )(seat, back, base)


def local(queries, kv_cache, new_kv, lengths, adapter_ids, place, ranks, w_out, a_store, b_store):
    request_count, step_count = (queries.shape[0], queries.shape[1])
    owners = lax.axis_size("store")
    cores = lax.axis_size("tensor")
    core = lax.axis_index("tensor")
    per_owner, feature_half, rank_width = a_store.shape
    out_half = b_store.shape[2]
    seats = owners * QCAP
    shifts = [[(k, (k + step) % cores) for k in range(cores)] for step in range(1, cores)]

    attended, sent, seat = attend(
        queries, kv_cache, new_kv, lengths, adapter_ids, place, owners, per_owner
    )
    got = lax.all_to_all(sent, "store", split_axis=0, concat_axis=0, tiled=True)

    blocks = [((core + step) % cores).reshape(1) for step in range(cores)]
    a_turned = jnp.swapaxes(a_store, 1, 2)
    here = (lax.axis_index("store") * per_owner).reshape(1)
    share, x, a_near, factor = other_columns(
        attended, w_out, blocks[1], out_half, here, place, ranks, a_turned
    )
    share = lax.ppermute(share, "tensor", shifts[0])

    own, slot = low(got, a_near, seats, step_count)
    others = jnp.stack([lax.ppermute(own, "tensor", shift) for shift in shifts])
    back = update(own, others, slot, factor, b_store, owners)
    back, x, share = lax.optimization_barrier((back, x, share))
    back = lax.all_to_all(back, "store", split_axis=0, concat_axis=0, tiled=True)
    for step in range(2, cores):
        more = own_columns(x, w_out, blocks[step], out_half, jnp.zeros_like(share))
        share = share + lax.ppermute(more, "tensor", shifts[step - 1])
    base = own_columns(x, w_out, blocks[0], out_half, share)
    return finish(seat, back, base, request_count, step_count)


def solution(mesh):
    return jax.shard_map(
        local,
        mesh=mesh,
        in_specs=(
            P(("rep", "store"), None, "tensor", None),
            P(None, ("rep", "store"), "tensor", None, None),
            P(None, ("rep", "store"), None, "tensor", None),
            P(("rep", "store")),
            P(("rep", "store")),
            P("rep"),
            P("rep"),
            P("tensor", None),
            P(("rep", "store"), "tensor", None),
            P(("rep", "store"), None, "tensor"),
        ),
        out_specs=P(("rep", "store"), None, "tensor"),
        check_vma=False,
    )
```
